256 devices in a mesh: dp: 64 (over x, z, core), mp: 4 (over y).
Axes of the slice: x: 4, y: 4, z: 8, core: 2. Of those that a mesh axis runs over, the one named last changes fastest.
Arguments:
- grad_in: bfloat16 [64, 192, 12288], P('dp', None, 'mp'), may hold values from -400000 to 400000
- grad_out: bfloat16 [64, 192, 12288], P('dp', None, 'mp'), may hold values from -400000 to 400000
- error_in: float32 [64, 192, 12288], P('dp', None, 'mp'), may hold values from -6 to 6
- error_out: float32 [64, 192, 12288], P('dp', None, 'mp'), may hold values from -6 to 6
- warm_in: float32 [192, 64], replicated, may hold values from -6 to 6
- warm_out: float32 [192, 64], replicated, may hold values from -6 to 6
- loss_scale: float32 [], replicated, may hold values from 1024 to 4096
Outputs:
- new_error_in: float32 [64, 192, 12288], P('dp', None, 'mp')
- new_error_out: float32 [64, 192, 12288], P('dp', None, 'mp')
- new_warm_in: float32 [192, 64], replicated
- new_warm_out: float32 [192, 64], replicated
The draws below stay inside these ranges and needn't reach their ends.
All inputs are finite; a program needn't handle non-finite values.
Results may differ from the reference program's by a relative error of at most 0.0003.
Values sent between devices are 32-bit elements; how exact they have to be, the bound alone decides.
A program may use at most 64 MiB of HBM per device.

```python
import math
import jax
import jax.numpy as jnp
from jax import lax

ROWS = 192
FF_WIN = 12288
RANK = 64
N_DP = 64
N_MP = 4


def scale_field(key, col_low, col_high, row_high):
    key_col, key_row = jax.random.split(key)
    replica = 2.0 ** (jnp.arange(N_DP, dtype=jnp.float32) / max(N_DP - 1, 1))
    block = (jnp.arange(FF_WIN) // (FF_WIN // N_MP)).astype(jnp.float32)
    slice_rise = 3.0 ** (0.5 * block / max(N_MP - 1, 1))
    column = jnp.exp(jax.random.uniform(key_col, (FF_WIN,), jnp.float32, math.log(col_low), math.log(col_high)))
    row_scale = jnp.exp(jax.random.uniform(key_row, (ROWS,), jnp.float32, 0.0, math.log(row_high)))
    return 2048.0 * replica[:, None, None] * row_scale[None, :, None] * (column * slice_rise)[None, None, :]


def draw_grad_in(key, part):
    key = jax.random.fold_in(key, 11)
    key_scale, key_base = jax.random.split(key, 2)
    shape = (N_DP, ROWS, FF_WIN)
    base = jnp.clip(jax.random.normal(key_base, shape, jnp.float32), -6.0, 6.0)
    scales = scale_field(key_scale, 0.3, 3.0, 3.0)
    return (base * scales).astype(jnp.bfloat16)


def draw_grad_out(key, part):
    key = jax.random.fold_in(key, 23)
    key_scale, key_base = jax.random.split(key, 2)
    shape = (N_DP, ROWS, FF_WIN)
    base = jnp.clip(jax.random.normal(key_base, shape, jnp.float32), -6.0, 6.0)
    scales = scale_field(key_scale, 0.3, 3.0, 3.0)
    return (base * scales).astype(jnp.bfloat16)


def level_of(own_key, extent, pieces, low, top_value):
    loudness = 1.0
    for axis_at, blocks in pieces:
        steps = jax.random.uniform(jax.random.fold_in(jax.random.fold_in(own_key, 6), axis_at), (blocks,), jnp.float32, low / len(pieces), top_value / len(pieces))
        loudness = loudness * jnp.repeat(jnp.exp(steps), extent[axis_at] // blocks).reshape((-1,) + (1,) * (len(extent) - 1 - axis_at))
    return loudness


def bell_draw(stream_key, dims, deviation, bound, cuts=(), held_as=jnp.bfloat16):
    gain = level_of(stream_key, dims, cuts, -0.22, 0.18) if cuts else 1.0
    drawn = jax.random.normal(stream_key, dims, jnp.float32) * deviation * gain
    return jnp.minimum(jnp.maximum(drawn, -bound), bound).astype(held_as)


def setup_inputs(seed: int = 0) -> dict:
    keys = jax.random.split(jax.random.key(seed), 8)
    return {
        "grad_in": draw_grad_in(jax.random.fold_in(keys[7], 71), 0),
        "grad_out": draw_grad_out(jax.random.fold_in(keys[7], 71), 0),
        "error_in": bell_draw(keys[2], (N_DP, ROWS, FF_WIN), 1.0, 6.0, ((0, 64), (2, 4)), jnp.float32),
        "error_out": bell_draw(keys[3], (N_DP, ROWS, FF_WIN), 1.0, 6.0, ((0, 64), (2, 4)), jnp.float32),
        "warm_in": bell_draw(keys[4], (ROWS, RANK), 1.0, 6.0, (), jnp.float32),
        "warm_out": bell_draw(keys[5], (ROWS, RANK), 1.0, 6.0, (), jnp.float32),
        "loss_scale": jnp.clip(jnp.exp(jax.random.uniform(keys[6], (), jnp.float32, math.log(1024.0), math.log(4096.0))), 1024.0, 4096.0),
    }


def compress_single_matrix(grad, error, warmstart_factor, loss_scale):
    gradient_plus_residual = grad.astype(jnp.float32) / loss_scale + error
    left_product = jnp.einsum('hb,the->be', warmstart_factor, gradient_plus_residual, precision=lax.Precision.HIGHEST)
    gram_matrix = jnp.dot(left_product.astype(jnp.float32), left_product.T.astype(jnp.float32), precision=lax.Precision.HIGHEST, preferred_element_type=jnp.float32)
    factor_low = jnp.linalg.cholesky(gram_matrix)
    orthonormal_factor = lax.linalg.triangular_solve(factor_low, left_product, left_side=True, lower=True)
    reduced_product = jnp.einsum('xmq,cq->mc', gradient_plus_residual, orthonormal_factor, precision=lax.Precision.HIGHEST)
    new_warm = reduced_product / N_DP
    update = jnp.dot(new_warm.astype(jnp.float32), orthonormal_factor.astype(jnp.float32), precision=lax.Precision.HIGHEST, preferred_element_type=jnp.float32)
    return (gradient_plus_residual - update[None], new_warm)

def reference(grad_in, grad_out, error_in, error_out, warm_in, warm_out, loss_scale):
    err_first, warm_first = compress_single_matrix(grad_in, error_in, warm_in, loss_scale)
    err_second, warmstart_factor_second = compress_single_matrix(grad_out, error_out, warm_out, loss_scale)
    return (err_first, err_second, warm_first, warmstart_factor_second)
```

```python
import functools
import itertools

import jax
import jax.numpy as jnp
from jax import lax
from jax.experimental import pallas as pl
from jax.experimental.pallas import tpu as pltpu
from jax.sharding import PartitionSpec as P

F32 = jnp.float32
BF16 = jnp.bfloat16
MESH = pl.DeviceIdType.MESH
NX = 4
CORES = 2


def halves(value):
    high = value.astype(BF16)
    return high, (value - high.astype(F32)).astype(BF16)


def dot(a, b, dim_a, dim_b):
    return lax.dot_general(
        a, b, (((dim_a,), (dim_b,)), ((), ())), preferred_element_type=F32
    )


def reciprocal_of(scale_ref):
    return 1.0 / jnp.full((1, 128), scale_ref[0, 0], F32)


def reduce_kernel(
    sizes,
    grad_in,
    grad_out,
    error_in,
    error_out,
    warm_in,
    warm_out,
    scale_ref,
    left_out,
    prod_out,
    inv_out,
    grads,
    errors,
    high,
    low,
    left,
    from_core,
    from_x,
    from_diag,
    from_z,
    full,
    gram,
    gram_all,
    prod,
    prod_rs,
    prod_x,
    prod_z,
    prod_full,
    elim,
    send_sems,
    recv_sems,
    load_sems,
    store_sems,
):
    ny, nz = sizes
    rows, cols = grads.shape[1:]
    rank = left.shape[1]
    half_rank = rank // CORES
    group = half_rank // NX
    half = cols // 2
    part = cols // nz
    owners = ny * CORES
    share = rows // owners

    dp = lax.axis_index("dp")
    y = lax.axis_index("mp")
    core = dp % CORES
    z = (dp // CORES) % nz
    x = dp // (CORES * nz)
    x1 = x + 1 - 2 * (x % 2)
    x3 = 3 - x
    x2 = (x + 2) % NX

    def at(x_=x, z_=z, core_=core, y_=y):
        return ((x_ * nz + z_) * CORES + core_, y_)

    owner = y * CORES + core

    def owner_at(k):
        o = (owner + k) % owners
        return o, at(core_=o % CORES, y_=o // CORES)

    loads = {}
    for m, (g, e) in enumerate(((grad_in, error_in), (grad_out, error_out))):
        for h in range(2):
            c = pl.ds(h * half, half)
            for a, (src, dst) in enumerate(((g, grads), (e, errors))):
                copy = pltpu.make_async_copy(
                    src.at[:, c], dst.at[m, :, c], load_sems.at[m, h, a]
                )
                copy.start()
                loads[m, h, a] = copy

    peers = [at(x_=(x + k) % NX) for k in range(1, NX)]
    peers += [at(z_=(z + k) % nz) for k in range(1, nz)]
    peers += [owner_at(k)[1] for k in range(1, owners)]
    barrier = pltpu.get_barrier_semaphore()
    for peer in peers:
        pl.semaphore_signal(barrier, inc=1, device_id=peer, device_id_type=MESH)

    number = itertools.count()
    sent = []

    def send(src, dst, device):
        n = next(number)
        copy = pltpu.make_async_remote_copy(
            src_ref=src,
            dst_ref=dst,
            send_sem=send_sems.at[n],
            recv_sem=recv_sems.at[n],
            device_id=device,
            device_id_type=MESH,
        )
        copy.start()
        sent.append(copy)
        return copy

    scale = reciprocal_of(scale_ref)[:, :1]

    def group_rows(g):
        return pl.ds(pl.multiple_of(core * half_rank + g * group, group), group)

    my_rows = pl.ds(pl.multiple_of(core * half_rank, half_rank), half_rank)
    other_rows = pl.ds(
        pl.multiple_of((1 - core) * half_rank, half_rank), half_rank
    )
    side = (pl.ds(0, half), pl.ds(half, half))

    def part_cols(z_):
        return pl.ds(pl.multiple_of(z_ * part, part), part)

    tile = min(512, half)
    depth = min(1024, cols)
    totals = [None, None]

    def stream(m):
        warm_high, warm_low = halves((warm_in, warm_out)[m][...])
        warm_both = jnp.concatenate([warm_high, warm_low], axis=1)
        exchanged = []
        for h in range(2):
            loads[m, h, 0].wait()
            loads[m, h, 1].wait()

            def make(t, carry, h=h):
                c = pl.ds(pl.multiple_of(h * half + t * tile, tile), tile)
                field = grads[m, :, c].astype(F32) * scale + errors[m, :, c]
                field_high, field_low = halves(field)
                high[m, 0:rows, c] = field_high
                low[m, 0:rows, c] = field_low
                both = dot(warm_both, field_high, 0, 0)
                left[m, :, c] = (
                    both[:rank]
                    + both[rank:]
                    + dot(warm_high, field_low, 0, 0)
                )
                return carry

            lax.fori_loop(0, half // tile, make, 0)
            if m == 0 and h == 0:
                pl.semaphore_wait(barrier, len(peers))
            exchanged.append(
                send(
                    left.at[m, other_rows, side[h]],
                    from_core.at[m, :, side[h]],
                    at(core_=1 - core),
                )
            )
        yield
        for h in range(2):
            exchanged[h].wait_recv()
            left[m, my_rows, side[h]] += from_core[m, :, side[h]]
        diag = [
            send(
                left.at[m, group_rows(x2), side[h]],
                from_diag.at[m, :, side[h]],
                at(x_=(x1, x3)[h]),
            )
            for h in range(2)
        ]
        near = [
            send(
                left.at[m, group_rows((x1, x3)[h]), side[h]],
                from_x.at[m, h, :, side[h]],
                at(x_=(x1, x3)[h]),
            )
            for h in range(2)
        ]
        yield
        for h in range(2):
            diag[h].wait_recv()
            g = group_rows((x3, x1)[h])
            left[m, g, side[h]] += from_diag[m, :, side[h]]
            near.append(
                send(
                    left.at[m, g, side[h]],
                    from_x.at[m, 1 - h, :, side[h]],
                    at(x_=(x3, x1)[h]),
                )
            )
        yield
        for copy in near:
            copy.wait_recv()
        mine = group_rows(x)
        left[m, mine, :] += from_x[m, 0] + from_x[m, 1]
        summed = [
            send(
                left.at[m, mine, part_cols((z + k) % nz)],
                from_z.at[m, k],
                at(z_=(z + k) % nz),
            )
            for k in range(1, nz)
        ]
        yield
        total = left[m, mine, part_cols(z)]
        for k in range(1, nz):
            summed[k - 1].wait_recv()
            total += from_z[m, k]
        full[m, mine, part_cols(z)] = total
        here = full.at[m, mine, part_cols(z)]
        spread = [send(here, here, at(z_=(z + k) % nz)) for k in range(1, nz)]
        yield
        for copy in spread:
            copy.wait_recv()
        gathered = {}
        for first in (0, 1):
            for n in range(2):
                h = 1 - n if first == 0 else n
                here = full.at[m, mine, side[h]]
                gathered[n, h] = send(here, here, at(x_=(x1, x3)[n]))
        yield
        for n in range(2):
            h = 1 - n
            gathered[n, h].wait_recv()
            here = full.at[m, group_rows((x1, x3)[n]), side[h]]
            gathered[2, h] = send(here, here, at(x_=(x3, x1)[n]))
        yield
        for n, h in ((0, 0), (1, 1), (2, 0), (2, 1)):
            gathered[n, h].wait_recv()
        here = full.at[m, my_rows, :]
        last = send(here, here, at(core_=1 - core))
        yield
        last.wait_recv()
        store = pltpu.make_async_copy(
            full.at[m], left_out.at[m], store_sems.at[m]
        )
        store.start()
        value_high, value_low = halves(full[m])
        high[m, rows : rows + rank, :] = value_high
        low[m, rows : rows + rank, :] = value_low
        total = jnp.zeros((rows + rank, 2 * rank), F32)
        for t in range(cols // depth):
            c = pl.ds(t * depth, depth)
            left_high = high[m, rows : rows + rank, c]
            left_low = low[m, rows : rows + rank, c]
            one = dot(
                high[m, :, c],
                jnp.concatenate([left_high, left_low], axis=0),
                1,
                1,
            )
            two = dot(
                low[m, :, c],
                jnp.concatenate([left_high, left_high], axis=0),
                1,
                1,
            )
            total += one + pltpu.roll(one, rank, 1) + two
        totals[m] = total
        store.wait()

    streams = [stream(0), stream(1)]
    while streams:
        for s in list(streams):
            try:
                next(s)
            except StopIteration:
                streams.remove(s)

    lane = lax.broadcasted_iota(jnp.int32, (1, 2 * rank), 1)
    packed = jnp.where(lane < rank, totals[0], totals[1])
    gram[...] = packed[rows:]
    gram_all[y] = packed[rows:]
    prod[...] = packed[:rows]
    gram_copies = [
        send(gram, gram_all.at[y], at(y_=(y + k) % ny)) for k in range(1, ny)
    ]

    def share_rows(o):
        return pl.ds(pl.multiple_of(o * share, share), share)

    rs_copies = []
    for k in range(1, owners):
        o, device = owner_at(k)
        rs_copies.append(send(prod.at[share_rows(o), :], prod_rs.at[k], device))

    for copy in gram_copies:
        copy.wait_recv()
    gram_sum = gram_all[0]
    for k in range(1, ny):
        gram_sum += gram_all[k]

    row = lax.broadcasted_iota(jnp.int32, (rank, 2 * rank), 0)
    col = lax.broadcasted_iota(jnp.int32, (rank, 2 * rank), 1)
    unit = jnp.where(col - rank == row, 1.0, 0.0).astype(F32)
    elim[0] = jnp.where(col < rank, gram_sum, unit)
    elim[1] = jnp.where(col < rank, pltpu.roll(gram_sum, rank, 1), unit)

    def step(k, carry):
        for m in range(2):
            value = elim[m]
            pivot_row = elim[m, pl.ds(k, 1), :]
            pick = col == k
            pivot_col = jnp.sum(
                jnp.where(pick, value, 0.0), axis=1, keepdims=True
            )
            pivot = jnp.sum(
                jnp.where(lane == k, pivot_row, 0.0), axis=1, keepdims=True
            )
            factor = jnp.where(row[:, :1] > k, pivot_col / pivot, 0.0)
            elim[m] = value - factor * pivot_row
        return carry

    cuts = [0, rank // 3, 2 * rank // 3, rank]

    def eliminate(n):
        lax.fori_loop(cuts[n], cuts[n + 1], step, 0)

    eliminate(0)
    total = prod[share_rows(owner), :]
    for k in range(1, owners):
        rs_copies[k - 1].wait_recv()
        total += prod_rs[k]
    prod_x[x] = total
    copies = [
        send(prod_x.at[x], prod_x.at[x], at(x_=(x + k) % NX))
        for k in range(1, NX)
    ]
    eliminate(1)
    for copy in copies:
        copy.wait_recv()
    total = prod_x[0]
    for k in range(1, NX):
        total += prod_x[k]
    prod_z[z] = total
    copies = [
        send(prod_z.at[z], prod_z.at[z], at(z_=(z + k) % nz))
        for k in range(1, nz)
    ]
    eliminate(2)
    for copy in copies:
        copy.wait_recv()
    total = prod_z[0]
    for k in range(1, nz):
        total += prod_z[k]
    prod_full[share_rows(owner), :] = total
    here = prod_full.at[share_rows(owner), :]
    copies = [send(here, here, owner_at(k)[1]) for k in range(1, owners)]

    scaled = []
    for m in range(2):
        value = elim[m]
        pivots = jnp.sum(
            jnp.where(row == col, value, 0.0), axis=1, keepdims=True
        )
        scaled.append(value / jnp.sqrt(pivots))
    inv_out[...] = jnp.where(
        lane < rank, pltpu.roll(scaled[0], rank, 1), scaled[1]
    )
    for copy in copies:
        copy.wait_recv()
    prod_out[...] = prod_full[...]
    for copy in sent:
        copy.wait_send()


def reduce_call(
    sizes, grad_in, grad_out, error_in, error_out, warm_in, warm_out, scale
):
    ny, nz = sizes
    rows, cols = grad_in.shape
    rank = warm_in.shape[1]
    half_rank = rank // CORES
    group = half_rank // NX
    owners = ny * CORES
    share = rows // owners
    any_spec = pl.BlockSpec(memory_space=pl.ANY)
    vmem = pl.BlockSpec(memory_space=pltpu.VMEM)
    smem = pl.BlockSpec(memory_space=pltpu.SMEM)
    count = 2 * (2 + 6 + 2 * (nz - 1) + 6 + 1)
    count += (ny - 1) + 2 * (owners - 1) + (NX - 1) + (nz - 1)
    return pl.pallas_call(
        functools.partial(reduce_kernel, sizes),
        out_shape=(
            jax.ShapeDtypeStruct((2, rank, cols), F32),
            jax.ShapeDtypeStruct((rows, 2 * rank), F32),
            jax.ShapeDtypeStruct((rank, 2 * rank), F32),
        ),
        in_specs=[any_spec] * 4 + [vmem, vmem, smem],
        out_specs=(any_spec, vmem, vmem),
        scratch_shapes=[
            pltpu.VMEM((2, rows, cols), BF16),
            pltpu.VMEM((2, rows, cols), F32),
            pltpu.VMEM((2, rows + rank, cols), BF16),
            pltpu.VMEM((2, rows + rank, cols), BF16),
            pltpu.VMEM((2, rank, cols), F32),
            pltpu.VMEM((2, half_rank, cols), F32),
            pltpu.VMEM((2, 2, group, cols), F32),
            pltpu.VMEM((2, group, cols), F32),
            pltpu.VMEM((2, nz, group, cols // nz), F32),
            pltpu.VMEM((2, rank, cols), F32),
            pltpu.VMEM((rank, 2 * rank), F32),
            pltpu.VMEM((ny, rank, 2 * rank), F32),
            pltpu.VMEM((rows, 2 * rank), F32),
            pltpu.VMEM((owners, share, 2 * rank), F32),
            pltpu.VMEM((NX, share, 2 * rank), F32),
            pltpu.VMEM((nz, share, 2 * rank), F32),
            pltpu.VMEM((rows, 2 * rank), F32),
            pltpu.VMEM((2, rank, 2 * rank), F32),
            pltpu.SemaphoreType.DMA((count,)),
            pltpu.SemaphoreType.DMA((count,)),
            pltpu.SemaphoreType.DMA((2, 2, 2)),
            pltpu.SemaphoreType.DMA((2,)),
        ],
        compiler_params=pltpu.CompilerParams(
            collective_id=0,
            has_side_effects=True,
            vmem_limit_bytes=40 * 1024 * 1024,
        ),
        name="reduce_left",
    )(grad_in, grad_out, error_in, error_out, warm_in, warm_out, scale)


def finish_kernel(
    replicas,
    grad_in,
    grad_out,
    error_in,
    error_out,
    left,
    prod,
    inv,
    scale_ref,
    new_error_in,
    new_error_out,
    new_warm_in,
    new_warm_out,
    factor,
):
    rank = left.shape[1]

    @pl.when(pl.program_id(0) == 0)
    def _():
        for m, out in enumerate((new_warm_in, new_warm_out)):
            lanes = slice(m * rank, (m + 1) * rank)
            inverse = inv[:, lanes]
            warm = (
                lax.dot_general(
                    prod[:, lanes],
                    inverse,
                    (((1,), (1,)), ((), ())),
                    precision=lax.Precision.HIGHEST,
                    preferred_element_type=F32,
                )
                / replicas
            )
            out[...] = warm
            applied = lax.dot_general(
                warm,
                inverse,
                (((1,), (0,)), ((), ())),
                precision=lax.Precision.HIGHEST,
                preferred_element_type=F32,
            )
            applied_high, applied_low = halves(applied)
            factor[m] = jnp.concatenate(
                [applied_high, applied_high, applied_low], axis=1
            )

    scale = reciprocal_of(scale_ref)[:, :1]
    for m, (g, e, out) in enumerate(
        ((grad_in, error_in, new_error_in), (grad_out, error_out, new_error_out))
    ):
        left_high, left_low = halves(left[m])
        stacked = jnp.concatenate([left_high, left_low, left_high], axis=0)
        field = g[...].astype(F32) * scale + e[...]
        out[...] = field - dot(factor[m], stacked, 1, 0)


def finish_call(
    replicas, grad_in, grad_out, error_in, error_out, left, prod, inv, scale
):
    rows, cols = grad_in.shape
    rank = left.shape[1]
    tile = min(512, cols)
    wide = pl.BlockSpec((rows, tile), lambda t: (0, t))
    vmem = pl.BlockSpec(memory_space=pltpu.VMEM)
    smem = pl.BlockSpec(memory_space=pltpu.SMEM)
    whole = pl.BlockSpec((rows, rank), lambda t: (0, 0))
    return pl.pallas_call(
        functools.partial(finish_kernel, replicas),
        grid=(cols // tile,),
        out_shape=(
            jax.ShapeDtypeStruct((rows, cols), F32),
            jax.ShapeDtypeStruct((rows, cols), F32),
            jax.ShapeDtypeStruct((rows, rank), F32),
            jax.ShapeDtypeStruct((rows, rank), F32),
        ),
        in_specs=[wide] * 4
        + [pl.BlockSpec((2, rank, tile), lambda t: (0, 0, t)), vmem, vmem, smem],
        out_specs=(wide, wide, whole, whole),
        scratch_shapes=[pltpu.VMEM((2, rows, 3 * rank), BF16)],
        compiler_params=pltpu.CompilerParams(
            vmem_limit_bytes=32 * 1024 * 1024,
        ),
        name="new_errors",
    )(grad_in, grad_out, error_in, error_out, left, prod, inv, scale)


def per_device(
    sizes, replicas, grad_in, grad_out, error_in, error_out, warm_in, warm_out, loss_scale
):
    wide = [a[0] for a in (grad_in, grad_out, error_in, error_out)]
    scale = loss_scale.reshape(1, 1)
    left, prod, inv = reduce_call(sizes, *wide, warm_in, warm_out, scale)
    err_in, err_out, new_in, new_out = finish_call(
        replicas, *wide, left, prod, inv, scale
    )
    return err_in[None], err_out[None], new_in, new_out


def solution(mesh):
    wide = P("dp", None, "mp")
    sizes = (mesh.shape["mp"], mesh.shape["dp"] // (NX * CORES))
    return jax.shard_map(
        functools.partial(per_device, sizes, float(mesh.shape["dp"])),
        mesh=mesh,
        in_specs=(wide, wide, wide, wide, P(), P(), P()),
        out_specs=(wide, wide, P(), P()),
        check_vma=False,
    )
```

```python
import functools
import itertools

import jax
import jax.numpy as jnp
from jax import lax
from jax.experimental import pallas as pl
from jax.experimental.pallas import tpu as pltpu
from jax.sharding import PartitionSpec as P

F32 = jnp.float32
BF16 = jnp.bfloat16
MESH = pl.DeviceIdType.MESH
NX = 4
CORES = 2


def halves(value):
    high = value.astype(BF16)
    return high, (value - high.astype(F32)).astype(BF16)


def dot(a, b, dim_a, dim_b):
    return lax.dot_general(
        a, b, (((dim_a,), (dim_b,)), ((), ())), preferred_element_type=F32
    )


def reciprocal_of(scale_ref):
    return 1.0 / jnp.full((1, 128), scale_ref[0, 0], F32)


def reduce_kernel(
    sizes,
    grad_in,
    grad_out,
    error_in,
    error_out,
    warm_in,
    warm_out,
    scale_ref,
    fields,
    left_out,
    prod_out,
    inv_out,
    grads,
    errors,
    warms,
    high,
    low,
    left,
    from_core,
    from_x,
    from_diag,
    from_z,
    full,
    gram,
    gram_all,
    prod,
    prod_rs,
    prod_x,
    prod_z,
    prod_full,
    elim,
    send_sems,
    recv_sems,
    load_sems,
    warm_sems,
):
    ny, nz = sizes
    rows, cols = grads.shape[1:]
    rank = left.shape[1]
    half_rank = rank // CORES
    group = half_rank // NX
    half = cols // 2
    part = cols // nz
    owners = ny * CORES
    share = rows // owners

    dp = lax.axis_index("dp")
    y = lax.axis_index("mp")
    core = dp % CORES
    z = (dp // CORES) % nz
    x = dp // (CORES * nz)
    x1 = x + 1 - 2 * (x % 2)
    x3 = 3 - x
    x2 = (x + 2) % NX

    def at(x_=x, z_=z, core_=core, y_=y):
        return ((x_ * nz + z_) * CORES + core_, y_)

    owner = y * CORES + core

    def owner_at(k):
        o = (owner + k) % owners
        return o, at(core_=o % CORES, y_=o // CORES)

    loads = {}
    for m, (g, e) in enumerate(((grad_in, error_in), (grad_out, error_out))):
        for h in range(2):
            c = pl.ds(h * half, half)
            for a, (src, dst) in enumerate(((g, grads), (e, errors))):
                copy = pltpu.make_async_copy(
                    src.at[:, c], dst.at[m, :, c], load_sems.at[m, h, a]
                )
                copy.start()
                loads[m, h, a] = copy

    for m, w in enumerate((warm_in, warm_out)):
        loads[m, "w"] = pltpu.make_async_copy(w, warms.at[m], warm_sems.at[m])
        loads[m, "w"].start()

    peers = [at(x_=(x + k) % NX) for k in range(1, NX)]
    peers += [at(z_=(z + k) % nz) for k in range(1, nz)]
    peers += [owner_at(k)[1] for k in range(1, owners)]
    barrier = pltpu.get_barrier_semaphore()
    for peer in peers:
        pl.semaphore_signal(barrier, inc=1, device_id=peer, device_id_type=MESH)

    number = itertools.count()
    sent = []

    def send(src, dst, device):
        n = next(number)
        copy = pltpu.make_async_remote_copy(
            src_ref=src,
            dst_ref=dst,
            send_sem=send_sems.at[n],
            recv_sem=recv_sems.at[n],
            device_id=device,
            device_id_type=MESH,
        )
        copy.start()
        sent.append(copy)
        return copy

    scale = reciprocal_of(scale_ref)[:, :1]

    def group_rows(g):
        return pl.ds(pl.multiple_of(core * half_rank + g * group, group), group)

    my_rows = pl.ds(pl.multiple_of(core * half_rank, half_rank), half_rank)
    other_rows = pl.ds(
        pl.multiple_of((1 - core) * half_rank, half_rank), half_rank
    )
    side = (pl.ds(0, half), pl.ds(half, half))

    def part_cols(z_):
        return pl.ds(pl.multiple_of(z_ * part, part), part)

    tile = min(512, half)
    depth = min(1024, cols)
    totals = [None, None]

    def stream(m):
        loads[m, "w"].wait()
        warm_high, warm_low = halves(warms[m])
        warm_both = jnp.concatenate([warm_high, warm_low], axis=0)
        exchanged = []
        for h in range(2):
            loads[m, h, 0].wait()
            loads[m, h, 1].wait()

            def make(t, carry, h=h):
                c = pl.ds(pl.multiple_of(h * half + t * tile, tile), tile)
                field = grads[m, :, c].astype(F32) * scale + errors[m, :, c]
                field_high, field_low = halves(field)
                fields[m, :, c] = field
                high[m, 0:rows, c] = field_high
                low[m, 0:rows, c] = field_low
                both = dot(warm_both, field_high, 1, 0)
                left[m, :, c] = (
                    both[:rank]
                    + both[rank:]
                    + dot(warm_high, field_low, 1, 0)
                )
                return carry

            lax.fori_loop(0, half // tile, make, 0)
            if m == 0 and h == 0:
                pl.semaphore_wait(barrier, len(peers))
            exchanged.append(
                send(
                    left.at[m, other_rows, side[h]],
                    from_core.at[m, :, side[h]],
                    at(core_=1 - core),
                )
            )
            yield
        diag, near = [], []
        for h in range(2):
            exchanged[h].wait_recv()
            left[m, my_rows, side[h]] += from_core[m, :, side[h]]
            neighbour = (x1, x3)[h]
            diag.append(
                send(
                    left.at[m, group_rows(x2), side[h]],
                    from_diag.at[m, :, side[h]],
                    at(x_=neighbour),
                )
            )
            near.append(
                send(
                    left.at[m, group_rows(neighbour), side[h]],
                    from_x.at[m, h, :, side[h]],
                    at(x_=neighbour),
                )
            )
            yield
        for h in range(2):
            diag[h].wait_recv()
            g = group_rows((x3, x1)[h])
            left[m, g, side[h]] += from_diag[m, :, side[h]]
            near.append(
                send(
                    left.at[m, g, side[h]],
                    from_x.at[m, 1 - h, :, side[h]],
                    at(x_=(x3, x1)[h]),
                )
            )
        yield
        for copy in near:
            copy.wait_recv()
        mine = group_rows(x)
        left[m, mine, :] += from_x[m, 0] + from_x[m, 1]
        summed = [
            send(
                left.at[m, mine, part_cols((z + k) % nz)],
                from_z.at[m, k],
                at(z_=(z + k) % nz),
            )
            for k in range(1, nz)
        ]
        yield
        total = left[m, mine, part_cols(z)]
        for k in range(1, nz):
            summed[k - 1].wait_recv()
            total += from_z[m, k]
        full[m, mine, part_cols(z)] = total
        here = full.at[m, mine, part_cols(z)]
        spread = [send(here, here, at(z_=(z + k) % nz)) for k in range(1, nz)]
        yield
        for copy in spread:
            copy.wait_recv()
        gathered = {}
        for first in (0, 1):
            for n in range(2):
                h = 1 - n if first == 0 else n
                here = full.at[m, mine, side[h]]
                gathered[n, h] = send(here, here, at(x_=(x1, x3)[n]))
        here = full.at[m, mine, :]
        shared = [send(here, here, at(core_=1 - core))]
        yield
        for n in range(2):
            h = 1 - n
            gathered[n, h].wait_recv()
            here = full.at[m, group_rows((x1, x3)[n]), side[h]]
            gathered[2, h] = send(here, here, at(x_=(x3, x1)[n]))
        yield
        for n in range(2):
            gathered[n, n].wait_recv()
            here = full.at[m, group_rows((x1, x3)[n]), :]
            shared.append(send(here, here, at(core_=1 - core)))
        for h in range(2):
            gathered[2, h].wait_recv()
            here = full.at[m, group_rows(x2), side[h]]
            shared.append(send(here, here, at(core_=1 - core)))
        yield
        for copy in shared:
            copy.wait_recv()
        value_high, value_low = halves(full[m])
        left_out[m, :rank] = value_high
        left_out[m, rank:] = value_low
        high[m, rows : rows + rank, :] = value_high
        low[m, rows : rows + rank, :] = value_low
        total = jnp.zeros((rows + rank, 2 * rank), F32)
        for t in range(cols // depth):
            c = pl.ds(t * depth, depth)
            left_high = high[m, rows : rows + rank, c]
            left_low = low[m, rows : rows + rank, c]
            one = dot(
                high[m, :, c],
                jnp.concatenate([left_high, left_low], axis=0),
                1,
                1,
            )
            two = dot(
                low[m, :, c],
                jnp.concatenate([left_high, left_high], axis=0),
                1,
                1,
            )
            total += one + pltpu.roll(one, rank, 1) + two
        totals[m] = total

    streams = (stream(0), stream(1))
    for m in (0, 0, 1, 0, 0, 1, 1, 0, 1, 0, 1, 1, 0, 1, 0, 1, 0, 1, 0, 0, 1, 1):
        next(streams[m], None)

    lane = lax.broadcasted_iota(jnp.int32, (1, 2 * rank), 1)
    packed = jnp.where(lane < rank, totals[0], totals[1])
    gram[...] = packed[rows:]
    gram_all[y] = packed[rows:]
    prod[...] = packed[:rows]
    gram_copies = [
        send(gram, gram_all.at[y], at(y_=(y + k) % ny)) for k in range(1, ny)
    ]

    def share_rows(o):
        return pl.ds(pl.multiple_of(o * share, share), share)

    rs_copies = []
    for k in range(1, owners):
        o, device = owner_at(k)
        rs_copies.append(send(prod.at[share_rows(o), :], prod_rs.at[k], device))

    total = prod[share_rows(owner), :]
    for k in range(1, owners):
        rs_copies[k - 1].wait_recv()
        total += prod_rs[k]
    prod_x[x] = total
    copies = [
        send(prod_x.at[x], prod_x.at[x], at(x_=(x + k) % NX))
        for k in range(1, NX)
    ]

    for copy in gram_copies:
        copy.wait_recv()
    gram_sum = gram_all[0]
    for k in range(1, ny):
        gram_sum += gram_all[k]

    row = lax.broadcasted_iota(jnp.int32, (rank, 2 * rank), 0)
    col = lax.broadcasted_iota(jnp.int32, (rank, 2 * rank), 1)
    unit = jnp.where(col - rank == row, 1.0, 0.0).astype(F32)
    elim[0] = jnp.where(col < rank, gram_sum, unit)
    elim[1] = jnp.where(col < rank, pltpu.roll(gram_sum, rank, 1), unit)

    def step(k, carry):
        for m in range(2):
            value = elim[m]
            pivot_row = elim[m, pl.ds(k, 1), :]
            pick = col == k
            pivot_col = jnp.sum(
                jnp.where(pick, value, 0.0), axis=1, keepdims=True
            )
            pivot = jnp.sum(
                jnp.where(lane == k, pivot_row, 0.0), axis=1, keepdims=True
            )
            factor = jnp.where(row[:, :1] > k, pivot_col / pivot, 0.0)
            elim[m] = value - factor * pivot_row
        return carry

    cuts = [0, 5 * rank // 16, 3 * rank // 4, rank]

    def eliminate(n):
        lax.fori_loop(cuts[n], cuts[n + 1], step, 0)

    eliminate(0)
    for copy in copies:
        copy.wait_recv()
    total = prod_x[0]
    for k in range(1, NX):
        total += prod_x[k]
    prod_z[z] = total
    copies = [
        send(prod_z.at[z], prod_z.at[z], at(z_=(z + k) % nz))
        for k in range(1, nz)
    ]
    eliminate(1)
    for copy in copies:
        copy.wait_recv()
    total = prod_z[0]
    for k in range(1, nz):
        total += prod_z[k]
    prod_full[share_rows(owner), :] = total
    here = prod_full.at[share_rows(owner), :]
    copies = [send(here, here, owner_at(k)[1]) for k in range(1, owners)]
    eliminate(2)

    scaled = []
    for m in range(2):
        value = elim[m]
        pivots = jnp.sum(
            jnp.where(row == col, value, 0.0), axis=1, keepdims=True
        )
        scaled.append(value / jnp.sqrt(pivots))
    inv_out[...] = jnp.where(
        lane < rank, pltpu.roll(scaled[0], rank, 1), scaled[1]
    )
    for copy in copies:
        copy.wait_recv()
    prod_out[...] = prod_full[...]
    for copy in sent:
        copy.wait_send()


def reduce_call(
    sizes, grad_in, grad_out, error_in, error_out, warm_in, warm_out, scale
):
    ny, nz = sizes
    rows, cols = grad_in.shape
    rank = warm_in.shape[0]
    half_rank = rank // CORES
    group = half_rank // NX
    owners = ny * CORES
    share = rows // owners
    hbm = pl.BlockSpec(memory_space=pltpu.HBM)
    vmem = pl.BlockSpec(memory_space=pltpu.VMEM)
    smem = pl.BlockSpec(memory_space=pltpu.SMEM)
    count = 2 * (2 + 6 + 2 * (nz - 1) + 6 + 5)
    count += (ny - 1) + 2 * (owners - 1) + (NX - 1) + (nz - 1)
    return pl.pallas_call(
        functools.partial(reduce_kernel, sizes),
        out_shape=(
            pltpu.VMEM((2, rows, cols), F32),
            pltpu.VMEM((2, 2 * rank, cols), BF16),
            pltpu.VMEM((rows, 2 * rank), F32),
            pltpu.VMEM((rank, 2 * rank), F32),
        ),
        in_specs=[hbm] * 6 + [smem],
        out_specs=(vmem,) * 4,
        scratch_shapes=[
            pltpu.VMEM((2, rows, cols), BF16),
            pltpu.VMEM((2, rows, cols), F32),
            pltpu.VMEM((2, rank, rows), F32),
            pltpu.VMEM((2, rows + rank, cols), BF16),
            pltpu.VMEM((2, rows + rank, cols), BF16),
            pltpu.VMEM((2, rank, cols), F32),
            pltpu.VMEM((2, half_rank, cols), F32),
            pltpu.VMEM((2, 2, group, cols), F32),
            pltpu.VMEM((2, group, cols), F32),
            pltpu.VMEM((2, nz, group, cols // nz), F32),
            pltpu.VMEM((2, rank, cols), F32),
            pltpu.VMEM((rank, 2 * rank), F32),
            pltpu.VMEM((ny, rank, 2 * rank), F32),
            pltpu.VMEM((rows, 2 * rank), F32),
            pltpu.VMEM((owners, share, 2 * rank), F32),
            pltpu.VMEM((NX, share, 2 * rank), F32),
            pltpu.VMEM((nz, share, 2 * rank), F32),
            pltpu.VMEM((rows, 2 * rank), F32),
            pltpu.VMEM((2, rank, 2 * rank), F32),
            pltpu.SemaphoreType.DMA((count,)),
            pltpu.SemaphoreType.DMA((count,)),
            pltpu.SemaphoreType.DMA((2, 2, 2)),
            pltpu.SemaphoreType.DMA((2,)),
        ],
        compiler_params=pltpu.CompilerParams(
            collective_id=0,
            has_side_effects=True,
            vmem_limit_bytes=40 * 1024 * 1024,
        ),
        name="reduce_left",
    )(grad_in, grad_out, error_in, error_out, warm_in, warm_out, scale)


def finish_kernel(
    replicas,
    fields,
    left,
    prod,
    inv,
    new_error_in,
    new_error_out,
    new_warm_in,
    new_warm_out,
    factor,
    made,
    store_sems,
):
    rows, cols = fields.shape[1:]
    rank = inv.shape[0]
    tile = made.shape[-1]
    exact = functools.partial(
        lax.dot_general,
        precision=lax.Precision.HIGHEST,
        preferred_element_type=F32,
    )
    stores = []
    for m, warm_out in enumerate((new_warm_in, new_warm_out)):
        lanes = slice(m * rank, (m + 1) * rank)
        inverse = inv[:, lanes]
        warm = exact(inverse, prod[:, lanes], (((1,), (1,)), ((), ()))) / replicas
        warm_out[...] = warm
        applied = exact(warm, inverse, (((0,), (0,)), ((), ())))
        applied_high, applied_low = halves(applied)
        factor[m] = jnp.concatenate(
            [applied_high, applied_high, applied_low], axis=1
        )
    for m, out in enumerate((new_error_in, new_error_out)):
        for t in range(cols // tile):
            c = pl.ds(t * tile, tile)
            stacked = jnp.concatenate([left[m, :, c], left[m, :rank, c]], axis=0)
            made[m, t] = fields[m, :, c] - dot(factor[m], stacked, 1, 0)
            store = pltpu.make_async_copy(
                made.at[m, t], out.at[:, c], store_sems.at[m, t]
            )
            store.start()
            stores.append(store)
    for store in stores:
        store.wait()


def finish_call(replicas, fields, left, prod, inv):
    rows, cols = fields.shape[1:]
    rank = inv.shape[0]
    tile = min(512, cols)
    vmem = pl.BlockSpec(memory_space=pltpu.VMEM)
    hbm = pl.BlockSpec(memory_space=pltpu.HBM)
    return pl.pallas_call(
        functools.partial(finish_kernel, replicas),
        out_shape=(
            jax.ShapeDtypeStruct((rows, cols), F32),
            jax.ShapeDtypeStruct((rows, cols), F32),
            jax.ShapeDtypeStruct((rank, rows), F32),
            jax.ShapeDtypeStruct((rank, rows), F32),
        ),
        in_specs=[vmem] * 4,
        out_specs=(hbm, hbm, vmem, vmem),
        scratch_shapes=[
            pltpu.VMEM((2, rows, 3 * rank), BF16),
            pltpu.VMEM((2, cols // tile, rows, tile), F32),
            pltpu.SemaphoreType.DMA((2, cols // tile)),
        ],
        compiler_params=pltpu.CompilerParams(
            vmem_limit_bytes=32 * 1024 * 1024,
        ),
        name="new_errors",
    )(fields, left, prod, inv)


def per_device(
    sizes, replicas, grad_in, grad_out, error_in, error_out, warm_in, warm_out, loss_scale
):
    wide = [
        pltpu.with_memory_space_constraint(a[0], pltpu.HBM)
        for a in (grad_in, grad_out, error_in, error_out)
    ]
    scale = loss_scale.reshape(1, 1)
    warms = [
        pltpu.with_memory_space_constraint(a.T, pltpu.HBM)
        for a in (warm_in, warm_out)
    ]
    reduced = reduce_call(sizes, *wide, *warms, scale)
    err_in, err_out, new_in, new_out = finish_call(replicas, *reduced)
    return err_in[None], err_out[None], new_in.T, new_out.T


def solution(mesh):
    wide = P("dp", None, "mp")
    sizes = (mesh.shape["mp"], mesh.shape["dp"] // (NX * CORES))
    return jax.shard_map(
        functools.partial(per_device, sizes, float(mesh.shape["dp"])),
        mesh=mesh,
        in_specs=(wide, wide, wide, wide, P(), P(), P()),
        out_specs=(wide, wide, P(), P()),
        check_vma=False,
    )
```

```python
import functools
import itertools

import jax
import jax.numpy as jnp
from jax import lax
from jax.experimental import pallas as pl
from jax.experimental.pallas import tpu as pltpu
from jax.sharding import PartitionSpec as P

F32 = jnp.float32
BF16 = jnp.bfloat16
MESH = pl.DeviceIdType.MESH
NX = 4
CORES = 2


def halves(value):
    high = value.astype(BF16)
    return high, (value - high.astype(F32)).astype(BF16)


def dot(a, b, dim_a, dim_b):
    return lax.dot_general(
        a, b, (((dim_a,), (dim_b,)), ((), ())), preferred_element_type=F32
    )


def reciprocal_of(scale_ref):
    return 1.0 / jnp.full((1, 128), scale_ref[0, 0], F32)


def reduce_kernel(
    sizes,
    grad_in,
    grad_out,
    error_in,
    error_out,
    warm_in,
    warm_out,
    scale_ref,
    fields,
    left_out,
    prod_out,
    inv_out,
    grads,
    errors,
    warms,
    high,
    low,
    left,
    left_other,
    left_core,
    from_core,
    from_x,
    from_diag,
    from_z,
    full,
    gram,
    gram_core,
    gram_all,
    prod,
    prod_rs,
    prod_x,
    prod_z,
    prod_full,
    elim,
    send_sems,
    recv_sems,
    load_sems,
    warm_sems,
):
    ny, nz = sizes
    rows, cols = grads.shape[1:]
    rank = left.shape[1]
    group = rank // NX
    half = cols // CORES
    piece = half // 2
    part_rows = from_z.shape[2]
    part = from_z.shape[3]
    across = half // part
    owners = ny * CORES
    share = rows // owners

    dp = lax.axis_index("dp")
    y = lax.axis_index("mp")
    core = dp % CORES
    z = (dp // CORES) % nz
    x = dp // (CORES * nz)
    x1 = x + 1 - 2 * (x % 2)
    x3 = 3 - x
    x2 = (x + 2) % NX

    def at(x_=x, z_=z, core_=core, y_=y):
        return ((x_ * nz + z_) * CORES + core_, y_)

    owner = y * CORES + core

    def owner_at(k):
        o = (owner + k) % owners
        return o, at(core_=o % CORES, y_=o // CORES)

    mine_at = core * half
    other_at = (1 - core) * half

    def columns(start, width):
        return pl.ds(pl.multiple_of(start, width), width)

    loads = {}
    for m, w in enumerate((warm_in, warm_out)):
        loads[m, "w"] = pltpu.make_async_copy(w, warms.at[m], warm_sems.at[m])
        loads[m, "w"].start()
    for m, (g, e) in enumerate(((grad_in, error_in), (grad_out, error_out))):
        for b, start in enumerate((other_at, mine_at)):
            for h in range(2):
                c = columns(start + h * piece, piece)
                for a, (src, dst) in enumerate(((g, grads), (e, errors))):
                    copy = pltpu.make_async_copy(
                        src.at[:, c], dst.at[m, :, c], load_sems.at[m, b, h, a]
                    )
                    copy.start()
                    loads[m, b, h, a] = copy

    peers = [at(x_=(x + k) % NX) for k in range(1, NX)]
    peers += [at(z_=(z + k) % nz) for k in range(1, nz)]
    peers += [owner_at(k)[1] for k in range(1, owners)]
    barrier = pltpu.get_barrier_semaphore()
    for peer in peers:
        pl.semaphore_signal(barrier, inc=1, device_id=peer, device_id_type=MESH)

    number = itertools.count()
    sent = []

    def send(src, dst, device):
        n = next(number)
        copy = pltpu.make_async_remote_copy(
            src_ref=src,
            dst_ref=dst,
            send_sem=send_sems.at[n],
            recv_sem=recv_sems.at[n],
            device_id=device,
            device_id_type=MESH,
        )
        copy.start()
        sent.append(copy)
        return copy

    scale = reciprocal_of(scale_ref)[:, :1]

    def group_rows(g):
        return pl.ds(pl.multiple_of(g * group, group), group)

    side = (pl.ds(0, piece), pl.ds(piece, piece))

    def full_side(h):
        return columns(mine_at + h * piece, piece)

    def part_rows_of(g, z_):
        start = g * group + z_ // across * part_rows
        return pl.ds(pl.multiple_of(start, part_rows), part_rows)

    def part_cols(z_, start=0):
        return columns(start + z_ % across * part, part)

    tile = min(384, piece)
    depth = min(768, half)
    totals = [None, None]
    shared = []

    def stream(m):
        exchanged = []
        loads[m, "w"].wait()
        warm_high, warm_low = halves(warms[m])
        warm_both = jnp.concatenate([warm_high, warm_low], axis=0)

        def make(b, h, out):
            loads[m, b, h, 0].wait()
            loads[m, b, h, 1].wait()
            start = (other_at, mine_at)[b] + h * piece

            def one(t, carry):
                c = columns(start + t * tile, tile)
                field = grads[m, :, c].astype(F32) * scale + errors[m, :, c]
                fields[m, :, c] = field
                field_high, field_low = halves(field)
                both = dot(warm_both, field_high, 1, 0)
                out[m, :, columns(h * piece + t * tile, tile)] = (
                    both[:rank]
                    + both[rank:]
                    + dot(warm_high, field_low, 1, 0)
                )
                return carry

            lax.fori_loop(0, piece // tile, one, 0)

        for h in range(2):
            make(0, h, left_other)
            if m == 0 and h == 0:
                pl.semaphore_wait(barrier, len(peers))
            exchanged.append(
                send(
                    left_other.at[m, :, side[h]],
                    left_core.at[m, :, side[h]],
                    at(core_=1 - core),
                )
            )
        yield
        for h in range(2):
            make(1, h, left)
        yield
        diag, near = [], []
        for h in range(2):
            exchanged[h].wait_recv()
            left[m, :, side[h]] += left_core[m, :, side[h]]
            neighbour = (x1, x3)[h]
            diag.append(
                send(
                    left.at[m, group_rows(x2), side[h]],
                    from_diag.at[m, :, side[h]],
                    at(x_=neighbour),
                )
            )
            near.append(
                send(
                    left.at[m, group_rows(neighbour), side[h]],
                    from_x.at[m, h, :, side[h]],
                    at(x_=neighbour),
                )
            )
            yield
        for h in range(2):
            diag[h].wait_recv()
            g = group_rows((x3, x1)[h])
            left[m, g, side[h]] += from_diag[m, :, side[h]]
            near.append(
                send(
                    left.at[m, g, side[h]],
                    from_x.at[m, 1 - h, :, side[h]],
                    at(x_=(x3, x1)[h]),
                )
            )
        other = send(
            fields.at[m, :, columns(other_at, half)],
            from_core.at[m],
            at(core_=1 - core),
        )
        yield
        for copy in near:
            copy.wait_recv()
        mine = group_rows(x)
        left[m, mine, :] += from_x[m, 0] + from_x[m, 1]
        summed = [
            send(
                left.at[m, part_rows_of(x, (z + k) % nz), part_cols((z + k) % nz)],
                from_z.at[m, k],
                at(z_=(z + k) % nz),
            )
            for k in range(1, nz)
        ]
        yield
        total = left[m, part_rows_of(x, z), part_cols(z)]
        for k in range(1, nz):
            summed[k - 1].wait_recv()
            total += from_z[m, k]
        full[m, part_rows_of(x, z), part_cols(z, mine_at)] = total
        here = full.at[m, part_rows_of(x, z), part_cols(z, mine_at)]
        spread = [send(here, here, at(z_=(z + k) % nz)) for k in range(1, nz)]
        other.wait_recv()

        def combine(t, carry):
            c = columns(t * tile, tile)
            field_high, field_low = halves(
                fields[m, :, columns(mine_at + t * tile, tile)]
                + from_core[m, :, c]
            )
            high[m, 0:rows, c] = field_high
            low[m, 0:rows, c] = field_low
            return carry

        lax.fori_loop(0, half // tile, combine, 0)
        yield
        for copy in spread:
            copy.wait_recv()
        gathered = {}
        for first in (0, 1):
            for n in range(2):
                h = 1 - n if first == 0 else n
                here = full.at[m, mine, full_side(h)]
                gathered[n, h] = send(here, here, at(x_=(x1, x3)[n]))
        yield
        for n in range(2):
            h = 1 - n
            gathered[n, h].wait_recv()
            here = full.at[m, group_rows((x1, x3)[n]), full_side(h)]
            gathered[2, h] = send(here, here, at(x_=(x3, x1)[n]))
        yield
        for n, h in ((0, 0), (1, 1), (2, 0), (2, 1)):
            gathered[n, h].wait_recv()
        c = columns(mine_at, half)
        here = full.at[m, :, c]
        shared.append(send(here, here, at(core_=1 - core)))
        value_high, value_low = halves(full[m, :, c])
        left_out[m, :rank, c] = value_high
        left_out[m, rank:, c] = value_low
        high[m, rows : rows + rank, :] = value_high
        low[m, rows : rows + rank, :] = value_low
        total = jnp.zeros((rows + rank, 2 * rank), F32)
        for t in range(half // depth):
            c = pl.ds(t * depth, depth)
            left_high = high[m, rows : rows + rank, c]
            left_low = low[m, rows : rows + rank, c]
            one = dot(
                high[m, :, c],
                jnp.concatenate([left_high, left_low], axis=0),
                1,
                1,
            )
            two = dot(
                low[m, :, c],
                jnp.concatenate([left_high, left_high], axis=0),
                1,
                1,
            )
            total += one + pltpu.roll(one, rank, 1) + two
        totals[m] = total

    streams = (stream(0), stream(1))
    for m in (0, 0, 1, 1, 0, 0, 1, 1) + (0, 1) * 6:
        next(streams[m], None)

    lane = lax.broadcasted_iota(jnp.int32, (1, 2 * rank), 1)
    packed = jnp.where(lane < rank, totals[0], totals[1])
    gram[...] = packed[rows:]
    prod[...] = packed[:rows]
    gram_pair = send(gram, gram_core, at(core_=1 - core))

    def share_rows(o):
        return pl.ds(pl.multiple_of(o * share, share), share)

    rs_copies = []
    for k in range(1, owners):
        o, device = owner_at(k)
        rs_copies.append(send(prod.at[share_rows(o), :], prod_rs.at[k], device))

    gram_pair.wait_recv()
    gram_all[y] = gram[...] + gram_core[...]
    gram_copies = [
        send(gram_all.at[y], gram_all.at[y], at(y_=(y + k) % ny))
        for k in range(1, ny)
    ]
    total = prod[share_rows(owner), :]
    for k in range(1, owners):
        rs_copies[k - 1].wait_recv()
        total += prod_rs[k]
    prod_x[x] = total
    copies = [
        send(prod_x.at[x], prod_x.at[x], at(x_=(x + k) % NX))
        for k in range(1, NX)
    ]

    for copy in gram_copies:
        copy.wait_recv()
    gram_sum = gram_all[0]
    for k in range(1, ny):
        gram_sum += gram_all[k]

    row = lax.broadcasted_iota(jnp.int32, (rank, 2 * rank), 0)
    col = lax.broadcasted_iota(jnp.int32, (rank, 2 * rank), 1)
    unit = jnp.where(col - rank == row, 1.0, 0.0).astype(F32)
    elim[0] = jnp.where(col < rank, gram_sum, unit)
    elim[1] = jnp.where(col < rank, pltpu.roll(gram_sum, rank, 1), unit)

    def entry(value, n):
        return jnp.sum(jnp.where(lane == n, value, 0.0), axis=1, keepdims=True)

    def step(j, carry):
        k = 2 * j
        for m in range(2):
            value = elim[m]
            row_one = elim[m, pl.ds(k, 1), :]
            row_two = elim[m, pl.ds(k + 1, 1), :]
            col_one, col_two = entry(value, k), entry(value, k + 1)
            pivot_one, above = entry(row_one, k), entry(row_one, k + 1)
            below, pivot_two = entry(row_two, k), entry(row_two, k + 1)
            inverse = 1.0 / pivot_one
            ratio = below * inverse
            row_two = row_two - ratio * row_one
            pivot_two = pivot_two - ratio * above
            one = jnp.where(row[:, :1] > k, col_one * inverse, 0.0)
            two = jnp.where(
                row[:, :1] > k + 1,
                (col_two - one * above) * (1.0 / pivot_two),
                0.0,
            )
            elim[m] = value - one * row_one - two * row_two
        return carry

    cuts = [0, 5 * rank // 32, 3 * rank // 8, rank // 2]

    def eliminate(n):
        lax.fori_loop(cuts[n], cuts[n + 1], step, 0)

    eliminate(0)
    for copy in copies:
        copy.wait_recv()
    total = prod_x[0]
    for k in range(1, NX):
        total += prod_x[k]
    prod_z[z] = total
    copies = [
        send(prod_z.at[z], prod_z.at[z], at(z_=(z + k) % nz))
        for k in range(1, nz)
    ]
    eliminate(1)
    for copy in copies:
        copy.wait_recv()
    total = prod_z[0]
    for k in range(1, nz):
        total += prod_z[k]
    prod_full[share_rows(owner), :] = total
    here = prod_full.at[share_rows(owner), :]
    copies = [send(here, here, owner_at(k)[1]) for k in range(1, owners)]
    eliminate(2)

    scaled = []
    for m in range(2):
        value = elim[m]
        pivots = jnp.sum(
            jnp.where(row == col, value, 0.0), axis=1, keepdims=True
        )
        scaled.append(value / jnp.sqrt(pivots))
    inv_out[:rank] = jnp.where(lane < rank, pltpu.roll(scaled[0], rank, 1), 0.0)
    inv_out[rank:] = jnp.where(lane < rank, 0.0, scaled[1])
    for m in range(2):
        shared[m].wait_recv()
        c = columns(other_at, half)
        value_high, value_low = halves(full[m, :, c])
        left_out[m, :rank, c] = value_high
        left_out[m, rank:, c] = value_low
    for copy in copies:
        copy.wait_recv()
    prod_out[...] = prod_full[...]
    for copy in sent:
        copy.wait_send()


def reduce_call(
    sizes, grad_in, grad_out, error_in, error_out, warm_in, warm_out, scale
):
    ny, nz = sizes
    rows, cols = grad_in.shape
    rank = warm_in.shape[0]
    group = rank // NX
    half = cols // CORES
    part_rows = 8
    part = half * group // (part_rows * nz)
    owners = ny * CORES
    share = rows // owners
    hbm = pl.BlockSpec(memory_space=pltpu.HBM)
    vmem = pl.BlockSpec(memory_space=pltpu.VMEM)
    smem = pl.BlockSpec(memory_space=pltpu.SMEM)
    count = 2 * (2 + 6 + 2 * (nz - 1) + 6 + 2) + 1
    count += (ny - 1) + 2 * (owners - 1) + (NX - 1) + (nz - 1)
    return pl.pallas_call(
        functools.partial(reduce_kernel, sizes),
        out_shape=(
            pltpu.VMEM((2, rows, cols), F32),
            pltpu.VMEM((2, 2 * rank, cols), BF16),
            pltpu.VMEM((rows, 2 * rank), F32),
            pltpu.VMEM((2 * rank, 2 * rank), F32),
        ),
        in_specs=[hbm] * 6 + [smem],
        out_specs=(vmem,) * 4,
        scratch_shapes=[
            pltpu.VMEM((2, rows, cols), BF16),
            pltpu.VMEM((2, rows, cols), F32),
            pltpu.VMEM((2, rank, rows), F32),
            pltpu.VMEM((2, rows + rank, half), BF16),
            pltpu.VMEM((2, rows + rank, half), BF16),
            pltpu.VMEM((2, rank, half), F32),
            pltpu.VMEM((2, rank, half), F32),
            pltpu.VMEM((2, rank, half), F32),
            pltpu.VMEM((2, rows, half), F32),
            pltpu.VMEM((2, 2, group, half), F32),
            pltpu.VMEM((2, group, half), F32),
            pltpu.VMEM((2, nz, part_rows, part), F32),
            pltpu.VMEM((2, rank, cols), F32),
            pltpu.VMEM((rank, 2 * rank), F32),
            pltpu.VMEM((rank, 2 * rank), F32),
            pltpu.VMEM((ny, rank, 2 * rank), F32),
            pltpu.VMEM((rows, 2 * rank), F32),
            pltpu.VMEM((owners, share, 2 * rank), F32),
            pltpu.VMEM((NX, share, 2 * rank), F32),
            pltpu.VMEM((nz, share, 2 * rank), F32),
            pltpu.VMEM((rows, 2 * rank), F32),
            pltpu.VMEM((2, rank, 2 * rank), F32),
            pltpu.SemaphoreType.DMA((count,)),
            pltpu.SemaphoreType.DMA((count,)),
            pltpu.SemaphoreType.DMA((2, 2, 2, 2)),
            pltpu.SemaphoreType.DMA((2,)),
        ],
        compiler_params=pltpu.CompilerParams(
            collective_id=0,
            has_side_effects=True,
            vmem_limit_bytes=40 * 1024 * 1024,
        ),
        name="reduce_left",
    )(grad_in, grad_out, error_in, error_out, warm_in, warm_out, scale)


def finish_kernel(
    replicas,
    fields,
    left,
    prod,
    inv,
    new_error_in,
    new_error_out,
    new_warm_in,
    new_warm_out,
    factor,
    made,
    store_sems,
):
    rows, cols = fields.shape[1:]
    rank = inv.shape[0] // 2
    tile = made.shape[-1]
    exact = functools.partial(
        lax.dot_general,
        precision=lax.Precision.HIGHEST,
        preferred_element_type=F32,
    )
    inverse = inv[...]
    product = prod[...] * (1.0 / replicas)
    warm = exact(product, inverse, (((1,), (1,)), ((), ())))
    applied = exact(warm, inverse, (((1,), (0,)), ((), ())))
    lane = lax.broadcasted_iota(jnp.int32, (1, 2 * rank), 1)
    for m in range(2):
        own = jnp.where(lane // rank == m, applied, 0.0)
        moved = pltpu.roll(own, rank, 1)
        twice = (own + moved).astype(BF16)
        rest = halves((own, moved)[m])[1]
        factor[m] = jnp.concatenate([twice, rest], axis=1)
    stores = []
    for m, out in enumerate((new_error_in, new_error_out)):
        for t in range(cols // tile):
            c = pl.ds(t * tile, tile)
            stacked = jnp.concatenate([left[m, :, c], left[m, :, c]], axis=0)
            made[m, t] = fields[m, :, c] - dot(factor[m], stacked, 1, 0)
            store = pltpu.make_async_copy(
                made.at[m, t], out.at[:, c], store_sems.at[m, t]
            )
            store.start()
            stores.append(store)
    both = exact(inverse, product, (((1,), (1,)), ((), ())))
    new_warm_in[...] = both[:rank]
    new_warm_out[...] = both[rank:]
    for store in stores:
        store.wait()


def finish_call(replicas, fields, left, prod, inv):
    rows, cols = fields.shape[1:]
    rank = inv.shape[0] // 2
    tile = min(512, cols)
    vmem = pl.BlockSpec(memory_space=pltpu.VMEM)
    hbm = pl.BlockSpec(memory_space=pltpu.HBM)
    return pl.pallas_call(
        functools.partial(finish_kernel, replicas),
        out_shape=(
            jax.ShapeDtypeStruct((rows, cols), F32),
            jax.ShapeDtypeStruct((rows, cols), F32),
            jax.ShapeDtypeStruct((rank, rows), F32),
            jax.ShapeDtypeStruct((rank, rows), F32),
        ),
        in_specs=[vmem] * 4,
        out_specs=(hbm, hbm, vmem, vmem),
        scratch_shapes=[
            pltpu.VMEM((2, rows, 4 * rank), BF16),
            pltpu.VMEM((2, cols // tile, rows, tile), F32),
            pltpu.SemaphoreType.DMA((2, cols // tile)),
        ],
        compiler_params=pltpu.CompilerParams(
            vmem_limit_bytes=32 * 1024 * 1024,
        ),
        name="new_errors",
    )(fields, left, prod, inv)


def per_device(
    sizes, replicas, grad_in, grad_out, error_in, error_out, warm_in, warm_out, loss_scale
):
    wide = [
        pltpu.with_memory_space_constraint(a[0], pltpu.HBM)
        for a in (grad_in, grad_out, error_in, error_out)
    ]
    scale = loss_scale.reshape(1, 1)
    warms = [
        pltpu.with_memory_space_constraint(a.T, pltpu.HBM)
        for a in (warm_in, warm_out)
    ]
    reduced = reduce_call(sizes, *wide, *warms, scale)
    err_in, err_out, new_in, new_out = finish_call(replicas, *reduced)
    return err_in[None], err_out[None], new_in.T, new_out.T


def solution(mesh):
    wide = P("dp", None, "mp")
    sizes = (mesh.shape["mp"], mesh.shape["dp"] // (NX * CORES))
    return jax.shard_map(
        functools.partial(per_device, sizes, float(mesh.shape["dp"])),
        mesh=mesh,
        in_specs=(wide, wide, wide, wide, P(), P(), P()),
        out_specs=(wide, wide, P(), P()),
        check_vma=False,
    )
```

```python
import functools
import itertools

import jax
import jax.numpy as jnp
from jax import lax
from jax.experimental import pallas as pl
from jax.experimental.pallas import tpu as pltpu
from jax.sharding import PartitionSpec as P

F32 = jnp.float32
BF16 = jnp.bfloat16
MESH = pl.DeviceIdType.MESH
NX = 4
CORES = 2


def halves(value):
    high = value.astype(BF16)
    return high, (value - high.astype(F32)).astype(BF16)


def dot(a, b, dim_a, dim_b):
    return lax.dot_general(
        a, b, (((dim_a,), (dim_b,)), ((), ())), preferred_element_type=F32
    )


def exact(a, b, dim_a, dim_b):
    return lax.dot_general(
        a,
        b,
        (((dim_a,), (dim_b,)), ((), ())),
        precision=lax.Precision.HIGHEST,
        preferred_element_type=F32,
    )


def farthest_first(n):
    return sorted(range(1, n), key=lambda k: -min(k, n - k))


def reciprocal_of(scale_ref):
    return 1.0 / jnp.full((1, 128), scale_ref[0, 0], F32)


def reduce_kernel(
    sizes,
    grad_in,
    grad_out,
    error_in,
    error_out,
    warm_in,
    warm_out,
    scale_ref,
    fields,
    left_out,
    prod_out,
    inv_out,
    grads,
    errors,
    warms,
    high,
    low,
    left,
    left_other,
    left_core,
    from_core,
    from_x,
    from_diag,
    from_z,
    full,
    gram,
    gram_core,
    gram_all,
    prod,
    prod_rs,
    prod_x,
    prod_z,
    prod_full,
    elim,
    send_sems,
    recv_sems,
    load_sems,
    warm_sems,
):
    ny, nz = sizes
    rows, cols = grads.shape[1:]
    rank = left.shape[1]
    group = rank // NX
    half = cols // CORES
    piece = half // 2
    part_rows = from_z.shape[2]
    part = from_z.shape[3]
    across = half // part
    owners = ny * CORES
    share = rows // owners

    dp = lax.axis_index("dp")
    y = lax.axis_index("mp")
    core = dp % CORES
    z = (dp // CORES) % nz
    x = dp // (CORES * nz)
    x1 = x + 1 - 2 * (x % 2)
    x3 = 3 - x
    x2 = (x + 2) % NX

    def at(x_=x, z_=z, core_=core, y_=y):
        return ((x_ * nz + z_) * CORES + core_, y_)

    owner = y * CORES + core

    def owner_at(k):
        o = (owner + k) % owners
        return o, at(core_=o % CORES, y_=o // CORES)

    peers = [at(z_=(z + k) % nz) for k in farthest_first(nz)]
    peers += [at(x_=(x + k) % NX) for k in farthest_first(NX)]
    peers += [owner_at(k)[1] for k in farthest_first(owners)]
    barrier = pltpu.get_barrier_semaphore()
    for peer in peers:
        pl.semaphore_signal(barrier, inc=1, device_id=peer, device_id_type=MESH)

    mine_at = core * half
    other_at = (1 - core) * half

    def columns(start, width):
        return pl.ds(pl.multiple_of(start, width), width)

    loads = {}
    for m, w in enumerate((warm_in, warm_out)):
        loads[m, "w"] = pltpu.make_async_copy(w, warms.at[m], warm_sems.at[m])
        loads[m, "w"].start()
    for m, (g, e) in enumerate(((grad_in, error_in), (grad_out, error_out))):
        for b, start in enumerate((other_at, mine_at)):
            for h in range(2):
                c = columns(start + h * piece, piece)
                for a, (src, dst) in enumerate(((g, grads), (e, errors))):
                    copy = pltpu.make_async_copy(
                        src.at[:, c], dst.at[m, :, c], load_sems.at[m, b, h, a]
                    )
                    copy.start()
                    loads[m, b, h, a] = copy

    number = itertools.count()
    sent = []

    def send(src, dst, device):
        n = next(number)
        copy = pltpu.make_async_remote_copy(
            src_ref=src,
            dst_ref=dst,
            send_sem=send_sems.at[n],
            recv_sem=recv_sems.at[n],
            device_id=device,
            device_id_type=MESH,
        )
        copy.start()
        sent.append(copy)
        return copy

    scale = reciprocal_of(scale_ref)[:, :1]

    def group_rows(g):
        return pl.ds(pl.multiple_of(g * group, group), group)

    side = (pl.ds(0, piece), pl.ds(piece, piece))

    def full_side(h):
        return columns(mine_at + h * piece, piece)

    def part_rows_of(g, z_):
        start = g * group + z_ // across * part_rows
        return pl.ds(pl.multiple_of(start, part_rows), part_rows)

    def part_cols(z_, start=0):
        return columns(start + z_ % across * part, part)

    tile = min(768, piece)
    depth = min(768, half)
    totals = [None, None]
    shared = []

    def stream(m):
        exchanged = []
        loads[m, "w"].wait()
        warm_high, warm_low = halves(warms[m])
        warm_both = jnp.concatenate([warm_high, warm_low], axis=0)

        def make(b, h, out):
            loads[m, b, h, 0].wait()
            loads[m, b, h, 1].wait()
            start = (other_at, mine_at)[b] + h * piece

            def one(t, carry):
                c = columns(start + t * tile, tile)
                field = grads[m, :, c].astype(F32) * scale + errors[m, :, c]
                fields[m, :, c] = field
                field_high, field_low = halves(field)
                both = dot(warm_both, field_high, 1, 0)
                out[m, :, columns(h * piece + t * tile, tile)] = (
                    both[:rank]
                    + both[rank:]
                    + dot(warm_high, field_low, 1, 0)
                )
                return carry

            lax.fori_loop(0, piece // tile, one, 0)

        for h in range(2):
            make(0, h, left_other)
            if m == 0 and h == 0:
                pl.semaphore_wait(barrier, len(peers))
            exchanged.append(
                send(
                    left_other.at[m, :, side[h]],
                    left_core.at[m, :, side[h]],
                    at(core_=1 - core),
                )
            )
        yield
        for h in range(2):
            make(1, h, left)
        yield
        diag, near = [], []
        for h in range(2):
            exchanged[h].wait_recv()
            left[m, :, side[h]] += left_core[m, :, side[h]]
            neighbour = (x1, x3)[h]
            diag.append(
                send(
                    left.at[m, group_rows(x2), side[h]],
                    from_diag.at[m, :, side[h]],
                    at(x_=neighbour),
                )
            )
            near.append(
                send(
                    left.at[m, group_rows(neighbour), side[h]],
                    from_x.at[m, h, :, side[h]],
                    at(x_=neighbour),
                )
            )
            yield
        for h in range(2):
            diag[h].wait_recv()
            g = group_rows((x3, x1)[h])
            left[m, g, side[h]] += from_diag[m, :, side[h]]
            near.append(
                send(
                    left.at[m, g, side[h]],
                    from_x.at[m, 1 - h, :, side[h]],
                    at(x_=(x3, x1)[h]),
                )
            )
        other = send(
            fields.at[m, :, columns(other_at, half)],
            from_core.at[m],
            at(core_=1 - core),
        )
        yield
        for copy in near:
            copy.wait_recv()
        mine = group_rows(x)
        left[m, mine, :] += from_x[m, 0] + from_x[m, 1]
        summed = [
            send(
                left.at[m, part_rows_of(x, (z + k) % nz), part_cols((z + k) % nz)],
                from_z.at[m, k],
                at(z_=(z + k) % nz),
            )
            for k in farthest_first(nz)
        ]
        yield
        for copy in summed:
            copy.wait_recv()
        total = left[m, part_rows_of(x, z), part_cols(z)]
        for k in range(1, nz):
            total += from_z[m, k]
        full[m, part_rows_of(x, z), part_cols(z, mine_at)] = total
        here = full.at[m, part_rows_of(x, z), part_cols(z, mine_at)]
        spread = [
            send(here, here, at(z_=(z + k) % nz)) for k in farthest_first(nz)
        ]
        other.wait_recv()

        def combine(t, carry):
            c = columns(t * tile, tile)
            field_high, field_low = halves(
                fields[m, :, columns(mine_at + t * tile, tile)]
                + from_core[m, :, c]
            )
            high[m, 0:rows, c] = field_high
            low[m, 0:rows, c] = field_low
            return carry

        lax.fori_loop(0, half // tile, combine, 0)
        yield
        for copy in spread:
            copy.wait_recv()
        gathered = {}
        for first in (0, 1):
            for n in range(2):
                h = 1 - n if first == 0 else n
                here = full.at[m, mine, full_side(h)]
                gathered[n, h] = send(here, here, at(x_=(x1, x3)[n]))
        yield
        for n in range(2):
            h = 1 - n
            gathered[n, h].wait_recv()
            here = full.at[m, group_rows((x1, x3)[n]), full_side(h)]
            gathered[2, h] = send(here, here, at(x_=(x3, x1)[n]))
        yield
        for n, h in ((0, 0), (1, 1), (2, 0), (2, 1)):
            gathered[n, h].wait_recv()
        c = columns(mine_at, half)
        value_high, value_low = halves(full[m, :, c])
        left_out[m, :rank, c] = value_high
        left_out[m, rank:, c] = value_low
        high[m, rows : rows + rank, :] = value_high
        low[m, rows : rows + rank, :] = value_low
        total = jnp.zeros((rows + rank, 2 * rank), F32)
        for t in range(half // depth):
            c = pl.ds(t * depth, depth)
            left_high = high[m, rows : rows + rank, c]
            left_low = low[m, rows : rows + rank, c]
            one = dot(
                high[m, :, c],
                jnp.concatenate([left_high, left_low], axis=0),
                1,
                1,
            )
            two = dot(
                low[m, :, c],
                jnp.concatenate([left_high, left_high], axis=0),
                1,
                1,
            )
            total += one + pltpu.roll(one, rank, 1) + two
        totals[m] = total

    streams = (stream(0), stream(1))
    for m in (0, 0, 1, 0, 0, 1, 1, 1) + (0, 1) * 6:
        next(streams[m], None)

    lane = lax.broadcasted_iota(jnp.int32, (1, 2 * rank), 1)
    packed = jnp.where(lane < rank, totals[0], totals[1])
    gram[...] = packed[rows:]
    prod[...] = packed[:rows]
    gram_pair = send(gram, gram_core, at(core_=1 - core))

    def share_rows(o):
        return pl.ds(pl.multiple_of(o * share, share), share)

    rs_copies = []
    for k in farthest_first(owners):
        o, device = owner_at(k)
        rs_copies.append(send(prod.at[share_rows(o), :], prod_rs.at[k], device))

    gram_pair.wait_recv()
    gram_all[y] = gram[...] + gram_core[...]
    gram_copies = [
        send(gram_all.at[y], gram_all.at[y], at(y_=(y + k) % ny))
        for k in farthest_first(ny)
    ]
    for copy in rs_copies:
        copy.wait_recv()
    total = prod[share_rows(owner), :]
    for k in range(1, owners):
        total += prod_rs[k]
    prod_x[x] = total
    copies = [
        send(prod_x.at[x], prod_x.at[x], at(x_=(x + k) % NX))
        for k in farthest_first(NX)
    ]

    for m in range(2):
        here = full.at[m, :, columns(mine_at, half)]
        shared.append(send(here, here, at(core_=1 - core)))

    for copy in gram_copies:
        copy.wait_recv()
    gram_sum = gram_all[0]
    for k in range(1, ny):
        gram_sum += gram_all[k]

    row = lax.broadcasted_iota(jnp.int32, (rank, 2 * rank), 0)
    col = lax.broadcasted_iota(jnp.int32, (rank, 2 * rank), 1)
    unit = jnp.where(col - rank == row, 1.0, 0.0).astype(F32)
    elim[0] = jnp.where(col < rank, gram_sum, unit)
    elim[1] = jnp.where(col < rank, pltpu.roll(gram_sum, rank, 1), unit)

    def entry(value, n):
        return jnp.sum(jnp.where(lane == n, value, 0.0), axis=1, keepdims=True)

    def step(j, carry):
        k = 2 * j
        for m in range(2):
            value = elim[m]
            row_one = elim[m, pl.ds(k, 1), :]
            row_two = elim[m, pl.ds(k + 1, 1), :]
            col_one, col_two = entry(value, k), entry(value, k + 1)
            pivot_one, above = entry(row_one, k), entry(row_one, k + 1)
            below, pivot_two = entry(row_two, k), entry(row_two, k + 1)
            inverse = 1.0 / pivot_one
            ratio = below * inverse
            row_two = row_two - ratio * row_one
            pivot_two = pivot_two - ratio * above
            one = jnp.where(row[:, :1] > k, col_one * inverse, 0.0)
            two = jnp.where(
                row[:, :1] > k + 1,
                (col_two - one * above) * (1.0 / pivot_two),
                0.0,
            )
            elim[m] = value - one * row_one - two * row_two
        return carry

    cuts = [0, 5 * rank // 32, 3 * rank // 8, rank // 2]

    def eliminate(n):
        lax.fori_loop(cuts[n], cuts[n + 1], step, 0)

    eliminate(0)
    for copy in copies:
        copy.wait_recv()
    total = prod_x[0]
    for k in range(1, NX):
        total += prod_x[k]
    prod_z[z] = total
    copies = [
        send(prod_z.at[z], prod_z.at[z], at(z_=(z + k) % nz))
        for k in farthest_first(nz)
    ]
    eliminate(1)
    for copy in copies:
        copy.wait_recv()
    total = prod_z[0]
    for k in range(1, nz):
        total += prod_z[k]
    prod_full[share_rows(owner), :] = total
    here = prod_full.at[share_rows(owner), :]
    copies = [send(here, here, owner_at(k)[1]) for k in farthest_first(owners)]
    eliminate(2)

    scaled = []
    for m in range(2):
        value = elim[m]
        pivots = jnp.sum(
            jnp.where(row == col, value, 0.0), axis=1, keepdims=True
        )
        scaled.append(value / jnp.sqrt(pivots))
    inverse = jnp.concatenate(
        [
            jnp.where(lane < rank, pltpu.roll(scaled[0], rank, 1), 0.0),
            jnp.where(lane < rank, 0.0, scaled[1]),
        ],
        axis=0,
    )
    inv_out[0] = inverse
    inv_out[1] = exact(inverse, inverse, 0, 0)
    for m in range(2):
        shared[m].wait_recv()
        c = columns(other_at, half)
        value_high, value_low = halves(full[m, :, c])
        left_out[m, :rank, c] = value_high
        left_out[m, rank:, c] = value_low
    for copy in copies:
        copy.wait_recv()
    prod_out[...] = prod_full[...]
    for copy in sent:
        copy.wait_send()


def reduce_call(
    sizes, grad_in, grad_out, error_in, error_out, warm_in, warm_out, scale
):
    ny, nz = sizes
    rows, cols = grad_in.shape
    rank = warm_in.shape[0]
    group = rank // NX
    half = cols // CORES
    part_rows = 8
    part = half * group // (part_rows * nz)
    owners = ny * CORES
    share = rows // owners
    hbm = pl.BlockSpec(memory_space=pltpu.HBM)
    vmem = pl.BlockSpec(memory_space=pltpu.VMEM)
    smem = pl.BlockSpec(memory_space=pltpu.SMEM)
    count = 2 * (2 + 6 + 2 * (nz - 1) + 6 + 2) + 1
    count += (ny - 1) + 2 * (owners - 1) + (NX - 1) + (nz - 1)
    return pl.pallas_call(
        functools.partial(reduce_kernel, sizes),
        out_shape=(
            pltpu.VMEM((2, rows, cols), F32),
            pltpu.VMEM((2, 2 * rank, cols), BF16),
            pltpu.VMEM((rows, 2 * rank), F32),
            pltpu.VMEM((2, 2 * rank, 2 * rank), F32),
        ),
        in_specs=[hbm] * 6 + [smem],
        out_specs=(vmem,) * 4,
        scratch_shapes=[
            pltpu.VMEM((2, rows, cols), BF16),
            pltpu.VMEM((2, rows, cols), F32),
            pltpu.VMEM((2, rank, rows), F32),
            pltpu.VMEM((2, rows + rank, half), BF16),
            pltpu.VMEM((2, rows + rank, half), BF16),
            pltpu.VMEM((2, rank, half), F32),
            pltpu.VMEM((2, rank, half), F32),
            pltpu.VMEM((2, rank, half), F32),
            pltpu.VMEM((2, rows, half), F32),
            pltpu.VMEM((2, 2, group, half), F32),
            pltpu.VMEM((2, group, half), F32),
            pltpu.VMEM((2, nz, part_rows, part), F32),
            pltpu.VMEM((2, rank, cols), F32),
            pltpu.VMEM((rank, 2 * rank), F32),
            pltpu.VMEM((rank, 2 * rank), F32),
            pltpu.VMEM((ny, rank, 2 * rank), F32),
            pltpu.VMEM((rows, 2 * rank), F32),
            pltpu.VMEM((owners, share, 2 * rank), F32),
            pltpu.VMEM((NX, share, 2 * rank), F32),
            pltpu.VMEM((nz, share, 2 * rank), F32),
            pltpu.VMEM((rows, 2 * rank), F32),
            pltpu.VMEM((2, rank, 2 * rank), F32),
            pltpu.SemaphoreType.DMA((count,)),
            pltpu.SemaphoreType.DMA((count,)),
            pltpu.SemaphoreType.DMA((2, 2, 2, 2)),
            pltpu.SemaphoreType.DMA((2,)),
        ],
        compiler_params=pltpu.CompilerParams(
            collective_id=0,
            has_side_effects=True,
            vmem_limit_bytes=40 * 1024 * 1024,
        ),
        name="reduce_left",
    )(grad_in, grad_out, error_in, error_out, warm_in, warm_out, scale)


def finish_kernel(
    replicas,
    fields,
    left,
    prod,
    inv,
    new_error_in,
    new_error_out,
    new_warm_in,
    new_warm_out,
    factor,
    made,
    store_sems,
):
    rows, cols = fields.shape[1:]
    rank = inv.shape[1] // 2
    tile = made.shape[-1]
    product = prod[...] * (1.0 / replicas)
    applied = exact(product, inv[1], 1, 0)
    lane = lax.broadcasted_iota(jnp.int32, (1, 2 * rank), 1)
    for m in range(2):
        own = jnp.where(lane // rank == m, applied, 0.0)
        moved = pltpu.roll(own, rank, 1)
        twice = (own + moved).astype(BF16)
        rest = halves((own, moved)[m])[1]
        factor[m] = jnp.concatenate([twice, rest], axis=1)
    stores = []
    for m, out in enumerate((new_error_in, new_error_out)):
        for t in range(cols // tile):
            c = pl.ds(t * tile, tile)
            stacked = jnp.concatenate([left[m, :, c], left[m, :, c]], axis=0)
            made[m, t] = fields[m, :, c] - dot(factor[m], stacked, 1, 0)
            store = pltpu.make_async_copy(
                made.at[m, t], out.at[:, c], store_sems.at[m, t]
            )
            store.start()
            stores.append(store)
    both = exact(inv[0], product, 1, 1)
    new_warm_in[...] = both[:rank]
    new_warm_out[...] = both[rank:]
    for store in stores:
        store.wait()


def finish_call(replicas, fields, left, prod, inv):
    rows, cols = fields.shape[1:]
    rank = inv.shape[1] // 2
    tile = min(512, cols)
    vmem = pl.BlockSpec(memory_space=pltpu.VMEM)
    hbm = pl.BlockSpec(memory_space=pltpu.HBM)
    return pl.pallas_call(
        functools.partial(finish_kernel, replicas),
        out_shape=(
            jax.ShapeDtypeStruct((rows, cols), F32),
            jax.ShapeDtypeStruct((rows, cols), F32),
            jax.ShapeDtypeStruct((rank, rows), F32),
            jax.ShapeDtypeStruct((rank, rows), F32),
        ),
        in_specs=[vmem] * 4,
        out_specs=(hbm, hbm, vmem, vmem),
        scratch_shapes=[
            pltpu.VMEM((2, rows, 4 * rank), BF16),
            pltpu.VMEM((2, cols // tile, rows, tile), F32),
            pltpu.SemaphoreType.DMA((2, cols // tile)),
        ],
        compiler_params=pltpu.CompilerParams(
            vmem_limit_bytes=32 * 1024 * 1024,
        ),
        name="new_errors",
    )(fields, left, prod, inv)


def per_device(
    sizes, replicas, grad_in, grad_out, error_in, error_out, warm_in, warm_out, loss_scale
):
    wide = [
        pltpu.with_memory_space_constraint(a[0], pltpu.HBM)
        for a in (grad_in, grad_out, error_in, error_out)
    ]
    scale = loss_scale.reshape(1, 1)
    warms = [
        pltpu.with_memory_space_constraint(a.T, pltpu.HBM)
        for a in (warm_in, warm_out)
    ]
    reduced = reduce_call(sizes, *wide, *warms, scale)
    err_in, err_out, new_in, new_out = finish_call(replicas, *reduced)
    return err_in[None], err_out[None], new_in.T, new_out.T


def solution(mesh):
    wide = P("dp", None, "mp")
    sizes = (mesh.shape["mp"], mesh.shape["dp"] // (NX * CORES))
    return jax.shard_map(
        functools.partial(per_device, sizes, float(mesh.shape["dp"])),
        mesh=mesh,
        in_specs=(wide, wide, wide, wide, P(), P(), P()),
        out_specs=(wide, wide, P(), P()),
        check_vma=False,
    )
```

```python
import functools
import itertools

import jax
import jax.numpy as jnp
from jax import lax
from jax.experimental import pallas as pl
from jax.experimental.pallas import tpu as pltpu
from jax.sharding import PartitionSpec as P

F32 = jnp.float32
BF16 = jnp.bfloat16
MESH = pl.DeviceIdType.MESH
NX = 4
CORES = 2


def halves(value):
    high = value.astype(BF16)
    return high, (value - high.astype(F32)).astype(BF16)


def dot(a, b, dim_a, dim_b):
    return lax.dot_general(
        a, b, (((dim_a,), (dim_b,)), ((), ())), preferred_element_type=F32
    )


def exact(a, b, dim_a, dim_b):
    return lax.dot_general(
        a,
        b,
        (((dim_a,), (dim_b,)), ((), ())),
        precision=lax.Precision.HIGHEST,
        preferred_element_type=F32,
    )


def farthest_first(n):
    return sorted(range(1, n), key=lambda k: -min(k, n - k))


def reciprocal_of(scale_ref):
    return 1.0 / jnp.full((1, 128), scale_ref[0, 0], F32)


def reduce_kernel(
    sizes,
    grad_in,
    grad_out,
    error_in,
    error_out,
    warm_in,
    warm_out,
    scale_ref,
    fields,
    left_out,
    prod_out,
    inv_out,
    grads,
    errors,
    warms,
    high,
    low,
    left,
    left_other,
    left_core,
    from_core,
    from_x,
    from_diag,
    from_z,
    full,
    gram,
    gram_core,
    gram_all,
    prod,
    prod_rs,
    prod_x,
    prod_z,
    prod_full,
    elim,
    send_sems,
    recv_sems,
    load_sems,
    warm_sems,
):
    ny, nz = sizes
    rows, cols = grads.shape[1:]
    rank = left.shape[1]
    group = rank // NX
    half = cols // CORES
    piece = half // 2
    part_rows = from_z.shape[2]
    part = from_z.shape[3]
    across = half // part
    owners = ny * CORES
    share = rows // owners

    dp = lax.axis_index("dp")
    y = lax.axis_index("mp")
    core = dp % CORES
    z = (dp // CORES) % nz
    x = dp // (CORES * nz)
    x1 = x + 1 - 2 * (x % 2)
    x3 = 3 - x
    x2 = (x + 2) % NX

    def at(x_=x, z_=z, core_=core, y_=y):
        return ((x_ * nz + z_) * CORES + core_, y_)

    owner = y * CORES + core

    def owner_at(k):
        o = (owner + k) % owners
        return o, at(core_=o % CORES, y_=o // CORES)

    peers = [at(z_=(z + k) % nz) for k in farthest_first(nz)]
    peers += [at(x_=(x + k) % NX) for k in farthest_first(NX)]
    peers += [owner_at(k)[1] for k in farthest_first(owners)]
    barrier = pltpu.get_barrier_semaphore()
    for peer in peers:
        pl.semaphore_signal(barrier, inc=1, device_id=peer, device_id_type=MESH)

    mine_at = core * half
    other_at = (1 - core) * half

    def columns(start, width):
        return pl.ds(pl.multiple_of(start, width), width)

    loads = {}
    for m, w in enumerate((warm_in, warm_out)):
        loads[m, "w"] = pltpu.make_async_copy(w, warms.at[m], warm_sems.at[m])
        loads[m, "w"].start()
    for m, (g, e) in enumerate(((grad_in, error_in), (grad_out, error_out))):
        for b, start in enumerate((other_at, mine_at)):
            for h in range(2):
                c = columns(start + h * piece, piece)
                for a, (src, dst) in enumerate(((g, grads), (e, errors))):
                    copy = pltpu.make_async_copy(
                        src.at[:, c], dst.at[m, :, c], load_sems.at[m, b, h, a]
                    )
                    copy.start()
                    loads[m, b, h, a] = copy

    number = itertools.count()
    sent = []

    def send(src, dst, device):
        n = next(number)
        copy = pltpu.make_async_remote_copy(
            src_ref=src,
            dst_ref=dst,
            send_sem=send_sems.at[n],
            recv_sem=recv_sems.at[n],
            device_id=device,
            device_id_type=MESH,
        )
        copy.start()
        sent.append(copy)
        return copy

    scale = reciprocal_of(scale_ref)[:, :1]

    def group_rows(g):
        return pl.ds(pl.multiple_of(g * group, group), group)

    side = (pl.ds(0, piece), pl.ds(piece, piece))

    def full_side(h):
        return columns(mine_at + h * piece, piece)

    def part_rows_of(g, z_):
        start = g * group + z_ // across * part_rows
        return pl.ds(pl.multiple_of(start, part_rows), part_rows)

    def part_cols(z_, start=0):
        return columns(start + z_ % across * part, part)

    tile = min(768, piece)
    depth = min(768, half)
    totals = [None, None]
    shared = []
    others = [None, None]

    def stream(m):
        exchanged = []
        loads[m, "w"].wait()
        warm_high, warm_low = halves(warms[m])
        warm_both = jnp.concatenate([warm_high, warm_low], axis=0)

        def make(b, h, out):
            loads[m, b, h, 0].wait()
            loads[m, b, h, 1].wait()
            start = (other_at, mine_at)[b] + h * piece

            def one(t, carry):
                c = columns(start + t * tile, tile)
                field = grads[m, :, c].astype(F32) * scale + errors[m, :, c]
                fields[m, :, c] = field
                field_high, field_low = halves(field)
                both = dot(warm_both, field_high, 1, 0)
                out[m, :, columns(h * piece + t * tile, tile)] = (
                    both[:rank]
                    + both[rank:]
                    + dot(warm_high, field_low, 1, 0)
                )
                return carry

            lax.fori_loop(0, piece // tile, one, 0)

        for h in range(2):
            make(0, h, left_other)
            if m == 0 and h == 0:
                pl.semaphore_wait(barrier, len(peers))
            exchanged.append(
                send(
                    left_other.at[m, :, side[h]],
                    left_core.at[m, :, side[h]],
                    at(core_=1 - core),
                )
            )
        yield
        for h in range(2):
            make(1, h, left)
        yield
        diag, near = [], []
        for h in range(2):
            exchanged[h].wait_recv()
            left[m, :, side[h]] += left_core[m, :, side[h]]
            neighbour = (x1, x3)[h]
            diag.append(
                send(
                    left.at[m, group_rows(x2), side[h]],
                    from_diag.at[m, :, side[h]],
                    at(x_=neighbour),
                )
            )
            near.append(
                send(
                    left.at[m, group_rows(neighbour), side[h]],
                    from_x.at[m, h, :, side[h]],
                    at(x_=neighbour),
                )
            )
            yield
        for h in range(2):
            diag[h].wait_recv()
            g = group_rows((x3, x1)[h])
            left[m, g, side[h]] += from_diag[m, :, side[h]]
            near.append(
                send(
                    left.at[m, g, side[h]],
                    from_x.at[m, 1 - h, :, side[h]],
                    at(x_=(x3, x1)[h]),
                )
            )
        others[m] = send(
            fields.at[m, :, columns(other_at, half)],
            from_core.at[m],
            at(core_=1 - core),
        )
        yield
        for copy in near:
            copy.wait_recv()
        mine = group_rows(x)
        left[m, mine, :] += from_x[m, 0] + from_x[m, 1]
        summed = [
            send(
                left.at[m, part_rows_of(x, (z + k) % nz), part_cols((z + k) % nz)],
                from_z.at[m, k],
                at(z_=(z + k) % nz),
            )
            for k in farthest_first(nz)
        ]
        yield
        for copy in summed:
            copy.wait_recv()
        total = left[m, part_rows_of(x, z), part_cols(z)]
        for k in range(1, nz):
            total += from_z[m, k]
        full[m, part_rows_of(x, z), part_cols(z, mine_at)] = total
        here = full.at[m, part_rows_of(x, z), part_cols(z, mine_at)]
        spread = [
            send(here, here, at(z_=(z + k) % nz)) for k in farthest_first(nz)
        ]
        yield
        for copy in spread:
            copy.wait_recv()
        gathered = {}
        for first in (0, 1):
            for n in range(2):
                h = 1 - n if first == 0 else n
                here = full.at[m, mine, full_side(h)]
                gathered[n, h] = send(here, here, at(x_=(x1, x3)[n]))
        yield
        for n in range(2):
            h = 1 - n
            gathered[n, h].wait_recv()
            here = full.at[m, group_rows((x1, x3)[n]), full_side(h)]
            gathered[2, h] = send(here, here, at(x_=(x3, x1)[n]))
        yield
        for n, h in ((0, 0), (1, 1), (2, 0), (2, 1)):
            gathered[n, h].wait_recv()
        c = columns(mine_at, half)
        value_high, value_low = halves(full[m, :, c])
        left_out[m, :rank, c] = value_high
        left_out[m, rank:, c] = value_low
        high[m, rows : rows + rank, :] = value_high
        low[m, rows : rows + rank, :] = value_low
        total = jnp.zeros((rows + rank, 2 * rank), F32)
        for t in range(half // depth):
            c = pl.ds(t * depth, depth)
            left_high = high[m, rows : rows + rank, c]
            left_low = low[m, rows : rows + rank, c]
            one = dot(
                high[m, :, c],
                jnp.concatenate([left_high, left_low], axis=0),
                1,
                1,
            )
            two = dot(
                low[m, :, c],
                jnp.concatenate([left_high, left_high], axis=0),
                1,
                1,
            )
            total += one + pltpu.roll(one, rank, 1) + two
        totals[m] = total

    def combine(m):
        others[m].wait_recv()

        def one(t, carry):
            c = columns(t * tile, tile)
            field_high, field_low = halves(
                fields[m, :, columns(mine_at + t * tile, tile)]
                + from_core[m, :, c]
            )
            high[m, 0:rows, c] = field_high
            low[m, 0:rows, c] = field_low
            return carry

        lax.fori_loop(0, half // tile, one, 0)

    streams = (stream(0), stream(1))

    def advance(order):
        for m in order:
            next(streams[m], None)

    advance((0, 0, 1, 0, 0, 1, 1, 1) + (0, 1) * 2)
    combine(0)
    advance((0, 1))
    combine(1)
    advance((0, 1) * 3)

    lane = lax.broadcasted_iota(jnp.int32, (1, 2 * rank), 1)
    packed = jnp.where(lane < rank, totals[0], totals[1])
    gram[...] = packed[rows:]
    prod[...] = packed[:rows]
    gram_pair = send(gram, gram_core, at(core_=1 - core))

    def share_rows(o):
        return pl.ds(pl.multiple_of(o * share, share), share)

    rs_copies = []
    for k in farthest_first(owners):
        o, device = owner_at(k)
        rs_copies.append(send(prod.at[share_rows(o), :], prod_rs.at[k], device))

    gram_pair.wait_recv()
    gram_all[y] = gram[...] + gram_core[...]
    gram_copies = [
        send(gram_all.at[y], gram_all.at[y], at(y_=(y + k) % ny))
        for k in farthest_first(ny)
    ]
    for copy in rs_copies:
        copy.wait_recv()
    total = prod[share_rows(owner), :]
    for k in range(1, owners):
        total += prod_rs[k]
    prod_x[x] = total
    copies = [
        send(prod_x.at[x], prod_x.at[x], at(x_=(x + k) % NX))
        for k in farthest_first(NX)
    ]

    for m in range(2):
        here = full.at[m, :, columns(mine_at, half)]
        shared.append(send(here, here, at(core_=1 - core)))

    for copy in gram_copies:
        copy.wait_recv()
    gram_sum = gram_all[0]
    for k in range(1, ny):
        gram_sum += gram_all[k]

    row = lax.broadcasted_iota(jnp.int32, (rank, 2 * rank), 0)
    col = lax.broadcasted_iota(jnp.int32, (rank, 2 * rank), 1)
    unit = jnp.where(col - rank == row, 1.0, 0.0).astype(F32)
    elim[0] = jnp.where(col < rank, gram_sum, unit)
    elim[1] = jnp.where(col < rank, pltpu.roll(gram_sum, rank, 1), unit)

    def entry(value, n):
        return jnp.sum(jnp.where(lane == n, value, 0.0), axis=1, keepdims=True)

    def step(j, carry):
        k = 2 * j
        for m in range(2):
            value = elim[m]
            row_one = elim[m, pl.ds(k, 1), :]
            row_two = elim[m, pl.ds(k + 1, 1), :]
            col_one, col_two = entry(value, k), entry(value, k + 1)
            pivot_one, above = entry(row_one, k), entry(row_one, k + 1)
            below, pivot_two = entry(row_two, k), entry(row_two, k + 1)
            inverse = 1.0 / pivot_one
            ratio = below * inverse
            row_two = row_two - ratio * row_one
            pivot_two = pivot_two - ratio * above
            one = jnp.where(row[:, :1] > k, col_one * inverse, 0.0)
            two = jnp.where(
                row[:, :1] > k + 1,
                (col_two - one * above) * (1.0 / pivot_two),
                0.0,
            )
            elim[m] = value - one * row_one - two * row_two
        return carry

    cuts = [0, 3 * rank // 64, 19 * rank // 64, rank // 2]

    def eliminate(n):
        lax.fori_loop(cuts[n], cuts[n + 1], step, 0)

    eliminate(0)
    for copy in copies:
        copy.wait_recv()
    total = prod_x[0]
    for k in range(1, NX):
        total += prod_x[k]
    prod_z[z] = total
    copies = [
        send(prod_z.at[z], prod_z.at[z], at(z_=(z + k) % nz))
        for k in farthest_first(nz)
    ]
    eliminate(1)
    early, sent[:] = sent[:], []
    for copy in early:
        copy.wait_send()
    for copy in copies:
        copy.wait_recv()
    total = prod_z[0]
    for k in range(1, nz):
        total += prod_z[k]
    prod_full[share_rows(owner), :] = total
    here = prod_full.at[share_rows(owner), :]
    copies = [send(here, here, owner_at(k)[1]) for k in farthest_first(owners)]
    eliminate(2)

    scaled = []
    for m in range(2):
        value = elim[m]
        pivots = jnp.sum(
            jnp.where(row == col, value, 0.0), axis=1, keepdims=True
        )
        scaled.append(value / jnp.sqrt(pivots))
    inverse = jnp.concatenate(
        [
            jnp.where(lane < rank, pltpu.roll(scaled[0], rank, 1), 0.0),
            jnp.where(lane < rank, 0.0, scaled[1]),
        ],
        axis=0,
    )
    inv_out[0] = inverse
    inv_out[1] = exact(inverse, inverse, 0, 0)
    for m in range(2):
        shared[m].wait_recv()
        c = columns(other_at, half)
        value_high, value_low = halves(full[m, :, c])
        left_out[m, :rank, c] = value_high
        left_out[m, rank:, c] = value_low
    for copy in copies:
        copy.wait_recv()
    prod_out[...] = prod_full[...]
    for copy in sent:
        copy.wait_send()


def reduce_call(
    sizes, grad_in, grad_out, error_in, error_out, warm_in, warm_out, scale
):
    ny, nz = sizes
    rows, cols = grad_in.shape
    rank = warm_in.shape[0]
    group = rank // NX
    half = cols // CORES
    part_rows = 8
    part = half * group // (part_rows * nz)
    owners = ny * CORES
    share = rows // owners
    hbm = pl.BlockSpec(memory_space=pltpu.HBM)
    vmem = pl.BlockSpec(memory_space=pltpu.VMEM)
    smem = pl.BlockSpec(memory_space=pltpu.SMEM)
    count = 2 * (2 + 6 + 2 * (nz - 1) + 6 + 2) + 1
    count += (ny - 1) + 2 * (owners - 1) + (NX - 1) + (nz - 1)
    return pl.pallas_call(
        functools.partial(reduce_kernel, sizes),
        out_shape=(
            pltpu.VMEM((2, rows, cols), F32),
            pltpu.VMEM((2, 2 * rank, cols), BF16),
            pltpu.VMEM((rows, 2 * rank), F32),
            pltpu.VMEM((2, 2 * rank, 2 * rank), F32),
        ),
        in_specs=[hbm] * 6 + [smem],
        out_specs=(vmem,) * 4,
        scratch_shapes=[
            pltpu.VMEM((2, rows, cols), BF16),
            pltpu.VMEM((2, rows, cols), F32),
            pltpu.VMEM((2, rank, rows), F32),
            pltpu.VMEM((2, rows + rank, half), BF16),
            pltpu.VMEM((2, rows + rank, half), BF16),
            pltpu.VMEM((2, rank, half), F32),
            pltpu.VMEM((2, rank, half), F32),
            pltpu.VMEM((2, rank, half), F32),
            pltpu.VMEM((2, rows, half), F32),
            pltpu.VMEM((2, 2, group, half), F32),
            pltpu.VMEM((2, group, half), F32),
            pltpu.VMEM((2, nz, part_rows, part), F32),
            pltpu.VMEM((2, rank, cols), F32),
            pltpu.VMEM((rank, 2 * rank), F32),
            pltpu.VMEM((rank, 2 * rank), F32),
            pltpu.VMEM((ny, rank, 2 * rank), F32),
            pltpu.VMEM((rows, 2 * rank), F32),
            pltpu.VMEM((owners, share, 2 * rank), F32),
            pltpu.VMEM((NX, share, 2 * rank), F32),
            pltpu.VMEM((nz, share, 2 * rank), F32),
            pltpu.VMEM((rows, 2 * rank), F32),
            pltpu.VMEM((2, rank, 2 * rank), F32),
            pltpu.SemaphoreType.DMA((count,)),
            pltpu.SemaphoreType.DMA((count,)),
            pltpu.SemaphoreType.DMA((2, 2, 2, 2)),
            pltpu.SemaphoreType.DMA((2,)),
        ],
        compiler_params=pltpu.CompilerParams(
            collective_id=0,
            has_side_effects=True,
            vmem_limit_bytes=40 * 1024 * 1024,
        ),
        name="reduce_left",
    )(grad_in, grad_out, error_in, error_out, warm_in, warm_out, scale)


def finish_kernel(
    replicas,
    fields,
    left,
    prod,
    inv,
    new_error_in,
    new_error_out,
    new_warm_in,
    new_warm_out,
    factor,
    made,
    warms,
    store_sems,
    warm_sems,
):
    rows, cols = fields.shape[1:]
    rank = inv.shape[1] // 2
    tile = made.shape[-1]
    product = prod[...] * (1.0 / replicas)
    applied = exact(product, inv[1], 1, 0)
    lane = lax.broadcasted_iota(jnp.int32, (1, 2 * rank), 1)
    for m in range(2):
        own = jnp.where(lane // rank == m, applied, 0.0)
        moved = pltpu.roll(own, rank, 1)
        twice = (own + moved).astype(BF16)
        rest = halves((own, moved)[m])[1]
        factor[m] = jnp.concatenate([twice, rest], axis=1)
    stores = []
    for m, out in enumerate((new_error_in, new_error_out)):
        if m == 1:
            both = exact(inv[0], product, 1, 1)
            for n, warm_out in enumerate((new_warm_in, new_warm_out)):
                warms[n] = both[n * rank : (n + 1) * rank]
                store = pltpu.make_async_copy(
                    warms.at[n], warm_out, warm_sems.at[n]
                )
                store.start()
                stores.append(store)
        for t in range(cols // tile):
            c = pl.ds(t * tile, tile)
            stacked = jnp.concatenate([left[m, :, c], left[m, :, c]], axis=0)
            made[m, t] = fields[m, :, c] - dot(factor[m], stacked, 1, 0)
            store = pltpu.make_async_copy(
                made.at[m, t], out.at[:, c], store_sems.at[m, t]
            )
            store.start()
            stores.append(store)
    for store in stores:
        store.wait()


def finish_call(replicas, fields, left, prod, inv):
    rows, cols = fields.shape[1:]
    rank = inv.shape[1] // 2
    tile = min(512, cols)
    vmem = pl.BlockSpec(memory_space=pltpu.VMEM)
    hbm = pl.BlockSpec(memory_space=pltpu.HBM)
    return pl.pallas_call(
        functools.partial(finish_kernel, replicas),
        out_shape=(
            jax.ShapeDtypeStruct((rows, cols), F32),
            jax.ShapeDtypeStruct((rows, cols), F32),
            jax.ShapeDtypeStruct((rank, rows), F32),
            jax.ShapeDtypeStruct((rank, rows), F32),
        ),
        in_specs=[vmem] * 4,
        out_specs=(hbm,) * 4,
        scratch_shapes=[
            pltpu.VMEM((2, rows, 4 * rank), BF16),
            pltpu.VMEM((2, cols // tile, rows, tile), F32),
            pltpu.VMEM((2, rank, rows), F32),
            pltpu.SemaphoreType.DMA((2, cols // tile)),
            pltpu.SemaphoreType.DMA((2,)),
        ],
        compiler_params=pltpu.CompilerParams(
            vmem_limit_bytes=32 * 1024 * 1024,
        ),
        name="new_errors",
    )(fields, left, prod, inv)


def per_device(
    sizes, replicas, grad_in, grad_out, error_in, error_out, warm_in, warm_out, loss_scale
):
    wide = [
        pltpu.with_memory_space_constraint(a[0], pltpu.HBM)
        for a in (grad_in, grad_out, error_in, error_out)
    ]
    scale = loss_scale.reshape(1, 1)
    warms = [
        pltpu.with_memory_space_constraint(a.T, pltpu.HBM)
        for a in (warm_in, warm_out)
    ]
    reduced = reduce_call(sizes, *wide, *warms, scale)
    err_in, err_out, new_in, new_out = finish_call(replicas, *reduced)
    return err_in[None], err_out[None], new_in.T, new_out.T


def solution(mesh):
    wide = P("dp", None, "mp")
    sizes = (mesh.shape["mp"], mesh.shape["dp"] // (NX * CORES))
    return jax.shard_map(
        functools.partial(per_device, sizes, float(mesh.shape["dp"])),
        mesh=mesh,
        in_specs=(wide, wide, wide, wide, P(), P(), P()),
        out_specs=(wide, wide, P(), P()),
        check_vma=False,
    )
```

```python
import functools
import itertools

import jax
import jax.numpy as jnp
from jax import lax
from jax.experimental import pallas as pl
from jax.experimental.pallas import tpu as pltpu
from jax.sharding import PartitionSpec as P

F32 = jnp.float32
BF16 = jnp.bfloat16
MESH = pl.DeviceIdType.MESH
NX = 4
CORES = 2


def halves(value):
    high = value.astype(BF16)
    return high, (value - high.astype(F32)).astype(BF16)


def dot(a, b, dim_a, dim_b):
    return lax.dot_general(
        a, b, (((dim_a,), (dim_b,)), ((), ())), preferred_element_type=F32
    )


def exact(a, b, dim_a, dim_b):
    return lax.dot_general(
        a,
        b,
        (((dim_a,), (dim_b,)), ((), ())),
        precision=lax.Precision.HIGHEST,
        preferred_element_type=F32,
    )


def farthest_first(n):
    return sorted(range(1, n), key=lambda k: -min(k, n - k))


def reciprocal_of(scale_ref):
    return 1.0 / jnp.full((1, 128), scale_ref[0, 0], F32)


def reduce_kernel(
    sizes,
    grad_in,
    grad_out,
    error_in,
    error_out,
    warm_in,
    warm_out,
    scale_ref,
    fields,
    left_out,
    prod_out,
    inv_out,
    grads,
    errors,
    warms,
    high,
    low,
    left,
    left_other,
    left_core,
    from_core,
    from_x,
    from_diag,
    from_z,
    full,
    gram,
    gram_core,
    gram_all,
    prod,
    prod_rs,
    prod_x,
    prod_z,
    prod_full,
    elim,
    send_sems,
    recv_sems,
    load_sems,
    warm_sems,
):
    ny, nz = sizes
    rows, cols = grads.shape[1:]
    rank = left.shape[1]
    group = rank // NX
    half = cols // CORES
    piece = half // 2
    part_rows = from_z.shape[2]
    part = from_z.shape[3]
    across = half // part
    owners = ny * CORES
    share = rows // owners

    dp = lax.axis_index("dp")
    y = lax.axis_index("mp")
    core = dp % CORES
    z = (dp // CORES) % nz
    x = dp // (CORES * nz)
    x1 = x + 1 - 2 * (x % 2)
    x3 = 3 - x
    x2 = (x + 2) % NX

    def at(x_=x, z_=z, core_=core, y_=y):
        return ((x_ * nz + z_) * CORES + core_, y_)

    owner = y * CORES + core

    def owner_at(k):
        o = (owner + k) % owners
        return o, at(core_=o % CORES, y_=o // CORES)

    peers = [at(z_=(z + k) % nz) for k in farthest_first(nz)]
    peers += [at(x_=(x + k) % NX) for k in farthest_first(NX)]
    peers += [owner_at(k)[1] for k in farthest_first(owners)]
    barrier = pltpu.get_barrier_semaphore()
    for peer in peers:
        pl.semaphore_signal(barrier, inc=1, device_id=peer, device_id_type=MESH)

    mine_at = core * half
    other_at = (1 - core) * half

    def columns(start, width):
        return pl.ds(pl.multiple_of(start, width), width)

    loads = {}
    for m, w in enumerate((warm_in, warm_out)):
        loads[m, "w"] = pltpu.make_async_copy(w, warms.at[m], warm_sems.at[m])
        loads[m, "w"].start()
    for m, (g, e) in enumerate(((grad_in, error_in), (grad_out, error_out))):
        for b, start in enumerate((other_at, mine_at)):
            for h in range(2):
                c = columns(start + h * piece, piece)
                for a, (src, dst) in enumerate(((g, grads), (e, errors))):
                    copy = pltpu.make_async_copy(
                        src.at[:, c], dst.at[m, :, c], load_sems.at[m, b, h, a]
                    )
                    copy.start()
                    loads[m, b, h, a] = copy

    number = itertools.count()
    sent = []

    def send(src, dst, device):
        n = next(number)
        copy = pltpu.make_async_remote_copy(
            src_ref=src,
            dst_ref=dst,
            send_sem=send_sems.at[n],
            recv_sem=recv_sems.at[n],
            device_id=device,
            device_id_type=MESH,
        )
        copy.start()
        sent.append(copy)
        return copy

    scale = reciprocal_of(scale_ref)[:, :1]

    def group_rows(g):
        return pl.ds(pl.multiple_of(g * group, group), group)

    side = (pl.ds(0, piece), pl.ds(piece, piece))

    def full_side(h):
        return columns(mine_at + h * piece, piece)

    def part_rows_of(g, z_):
        start = g * group + z_ // across * part_rows
        return pl.ds(pl.multiple_of(start, part_rows), part_rows)

    def part_cols(z_, start=0):
        return columns(start + z_ % across * part, part)

    tile = min(768, piece)
    depth = min(384, half)
    totals = [None, None]
    shared = []
    others = [None, None]

    def stream(m):
        exchanged = []
        loads[m, "w"].wait()
        warm_high, warm_low = halves(warms[m])
        warm_both = jnp.concatenate([warm_high, warm_low], axis=0)

        def make(b, h, out):
            loads[m, b, h, 0].wait()
            loads[m, b, h, 1].wait()
            start = (other_at, mine_at)[b] + h * piece

            def one(t, carry):
                c = columns(start + t * tile, tile)
                field = grads[m, :, c].astype(F32) * scale + errors[m, :, c]
                fields[m, :, c] = field
                field_high, field_low = halves(field)
                both = dot(warm_both, field_high, 1, 0)
                out[m, :, columns(h * piece + t * tile, tile)] = (
                    both[:rank]
                    + both[rank:]
                    + dot(warm_high, field_low, 1, 0)
                )
                return carry

            lax.fori_loop(0, piece // tile, one, 0)

        for h in range(2):
            make(0, h, left_other)
            if m == 0 and h == 0:
                pl.semaphore_wait(barrier, len(peers))
            exchanged.append(
                send(
                    left_other.at[m, :, side[h]],
                    left_core.at[m, :, side[h]],
                    at(core_=1 - core),
                )
            )
        yield
        for h in range(2):
            make(1, h, left)
        yield
        diag, near = [], []
        for h in range(2):
            exchanged[h].wait_recv()
            left[m, :, side[h]] += left_core[m, :, side[h]]
            neighbour = (x1, x3)[h]
            diag.append(
                send(
                    left.at[m, group_rows(x2), side[h]],
                    from_diag.at[m, :, side[h]],
                    at(x_=neighbour),
                )
            )
            near.append(
                send(
                    left.at[m, group_rows(neighbour), side[h]],
                    from_x.at[m, h, :, side[h]],
                    at(x_=neighbour),
                )
            )
            yield
        for h in range(2):
            diag[h].wait_recv()
            g = group_rows((x3, x1)[h])
            left[m, g, side[h]] += from_diag[m, :, side[h]]
            near.append(
                send(
                    left.at[m, g, side[h]],
                    from_x.at[m, 1 - h, :, side[h]],
                    at(x_=(x3, x1)[h]),
                )
            )
        others[m] = send(
            fields.at[m, :, columns(other_at, half)],
            from_core.at[m],
            at(core_=1 - core),
        )
        yield
        for copy in near:
            copy.wait_recv()
        mine = group_rows(x)
        left[m, mine, :] += from_x[m, 0] + from_x[m, 1]
        summed = [
            send(
                left.at[m, part_rows_of(x, (z + k) % nz), part_cols((z + k) % nz)],
                from_z.at[m, k],
                at(z_=(z + k) % nz),
            )
            for k in farthest_first(nz)
        ]
        yield
        for copy in summed:
            copy.wait_recv()
        total = left[m, part_rows_of(x, z), part_cols(z)]
        for k in range(1, nz):
            total += from_z[m, k]
        full[m, part_rows_of(x, z), part_cols(z, mine_at)] = total
        here = full.at[m, part_rows_of(x, z), part_cols(z, mine_at)]
        spread = [
            send(here, here, at(z_=(z + k) % nz)) for k in farthest_first(nz)
        ]
        yield
        for copy in spread:
            copy.wait_recv()
        gathered = {}
        for first in (0, 1):
            for n in range(2):
                h = 1 - n if first == 0 else n
                here = full.at[m, mine, full_side(h)]
                gathered[n, h] = send(here, here, at(x_=(x1, x3)[n]))
        yield
        for n in range(2):
            h = 1 - n
            gathered[n, h].wait_recv()
            here = full.at[m, group_rows((x1, x3)[n]), full_side(h)]
            gathered[2, h] = send(here, here, at(x_=(x3, x1)[n]))
        yield
        for n, h in ((0, 0), (1, 1), (2, 0), (2, 1)):
            gathered[n, h].wait_recv()
        c = columns(mine_at, half)
        value_high, value_low = halves(full[m, :, c])
        left_out[m, :rank, c] = value_high
        left_out[m, rank:, c] = value_low
        high[m, rows : rows + rank, :] = value_high
        low[m, rows : rows + rank, :] = value_low
        total = jnp.zeros((rows + rank, 2 * rank), F32)
        for t in range(half // depth):
            c = pl.ds(t * depth, depth)
            left_high = high[m, rows : rows + rank, c]
            left_low = low[m, rows : rows + rank, c]
            one = dot(
                high[m, :, c],
                jnp.concatenate([left_high, left_low], axis=0),
                1,
                1,
            )
            two = dot(
                low[m, :, c],
                jnp.concatenate([left_high, left_high], axis=0),
                1,
                1,
            )
            total += one + pltpu.roll(one, rank, 1) + two
        totals[m] = total

    def combine(m):
        others[m].wait_recv()

        def one(t, carry):
            c = columns(t * tile, tile)
            field_high, field_low = halves(
                fields[m, :, columns(mine_at + t * tile, tile)]
                + from_core[m, :, c]
            )
            high[m, 0:rows, c] = field_high
            low[m, 0:rows, c] = field_low
            return carry

        lax.fori_loop(0, half // tile, one, 0)

    streams = (stream(0), stream(1))

    def advance(order):
        for m in order:
            next(streams[m], None)

    advance((0, 0, 1, 0, 0, 1, 1, 1) + (0, 1) * 2)
    combine(0)
    advance((0, 1))
    combine(1)
    advance((0, 1) * 3)

    lane = lax.broadcasted_iota(jnp.int32, (1, 2 * rank), 1)
    packed = jnp.where(lane < rank, totals[0], totals[1])
    gram[...] = packed[rows:]
    prod[...] = packed[:rows]

    def share_rows(o):
        return pl.ds(pl.multiple_of(o * share, share), share)

    rs_copies = []
    for k in farthest_first(owners):
        o, device = owner_at(k)
        rs_copies.append(send(prod.at[share_rows(o), :], prod_rs.at[k], device))

    gram_pair = send(gram, gram_core, at(core_=1 - core))
    gram_pair.wait_recv()
    gram_all[y] = gram[...] + gram_core[...]
    gram_copies = [
        send(gram_all.at[y], gram_all.at[y], at(y_=(y + k) % ny))
        for k in farthest_first(ny)
    ]
    for copy in rs_copies:
        copy.wait_recv()
    total = prod[share_rows(owner), :]
    for k in range(1, owners):
        total += prod_rs[k]
    prod_x[x] = total
    copies = [
        send(prod_x.at[x], prod_x.at[x], at(x_=(x + k) % NX))
        for k in farthest_first(NX)
    ]

    for m in range(2):
        here = full.at[m, :, columns(mine_at, half)]
        shared.append(send(here, here, at(core_=1 - core)))

    for copy in gram_copies:
        copy.wait_recv()
    gram_sum = gram_all[0]
    for k in range(1, ny):
        gram_sum += gram_all[k]

    row = lax.broadcasted_iota(jnp.int32, (rank, 2 * rank), 0)
    col = lax.broadcasted_iota(jnp.int32, (rank, 2 * rank), 1)
    unit = jnp.where(col - rank == row, 1.0, 0.0).astype(F32)
    elim[0] = jnp.where(col < rank, gram_sum, unit)
    elim[1] = jnp.where(col < rank, pltpu.roll(gram_sum, rank, 1), unit)

    def entry(value, n):
        return jnp.sum(jnp.where(lane == n, value, 0.0), axis=1, keepdims=True)

    def step(j, carry):
        k = 2 * j
        for m in range(2):
            value = elim[m]
            row_one = elim[m, pl.ds(k, 1), :]
            row_two = elim[m, pl.ds(k + 1, 1), :]
            col_one, col_two = entry(value, k), entry(value, k + 1)
            pivot_one, above = entry(row_one, k), entry(row_one, k + 1)
            below, pivot_two = entry(row_two, k), entry(row_two, k + 1)
            inverse = 1.0 / pivot_one
            ratio = below * inverse
            row_two = row_two - ratio * row_one
            pivot_two = pivot_two - ratio * above
            one = jnp.where(row[:, :1] > k, col_one * inverse, 0.0)
            two = jnp.where(
                row[:, :1] > k + 1,
                (col_two - one * above) * (1.0 / pivot_two),
                0.0,
            )
            elim[m] = value - one * row_one - two * row_two
        return carry

    cuts = [0, 3 * rank // 64, 19 * rank // 64, rank // 2]

    def eliminate(n):
        lax.fori_loop(cuts[n], cuts[n + 1], step, 0)

    eliminate(0)
    for copy in copies:
        copy.wait_recv()
    total = prod_x[0]
    for k in range(1, NX):
        total += prod_x[k]
    prod_z[z] = total
    copies = [
        send(prod_z.at[z], prod_z.at[z], at(z_=(z + k) % nz))
        for k in farthest_first(nz)
    ]
    eliminate(1)
    early, sent[:] = sent[:], []
    for copy in early:
        copy.wait_send()
    for copy in copies:
        copy.wait_recv()
    total = prod_z[0]
    for k in range(1, nz):
        total += prod_z[k]
    prod_full[share_rows(owner), :] = total
    here = prod_full.at[share_rows(owner), :]
    copies = [send(here, here, owner_at(k)[1]) for k in farthest_first(owners)]
    eliminate(2)

    scaled = []
    for m in range(2):
        value = elim[m]
        pivots = jnp.sum(
            jnp.where(row == col, value, 0.0), axis=1, keepdims=True
        )
        scaled.append(value / jnp.sqrt(pivots))
    inverse = jnp.concatenate(
        [
            jnp.where(lane < rank, pltpu.roll(scaled[0], rank, 1), 0.0),
            jnp.where(lane < rank, 0.0, scaled[1]),
        ],
        axis=0,
    )
    inv_out[0] = inverse
    inv_out[1] = exact(inverse, inverse, 0, 0)
    for m in range(2):
        shared[m].wait_recv()
        c = columns(other_at, half)
        value_high, value_low = halves(full[m, :, c])
        left_out[m, :rank, c] = value_high
        left_out[m, rank:, c] = value_low
    for copy in copies:
        copy.wait_recv()
    prod_out[...] = prod_full[...]
    for copy in sent:
        copy.wait_send()


def reduce_call(
    sizes, grad_in, grad_out, error_in, error_out, warm_in, warm_out, scale
):
    ny, nz = sizes
    rows, cols = grad_in.shape
    rank = warm_in.shape[0]
    group = rank // NX
    half = cols // CORES
    part_rows = 8
    part = half * group // (part_rows * nz)
    owners = ny * CORES
    share = rows // owners
    hbm = pl.BlockSpec(memory_space=pltpu.HBM)
    vmem = pl.BlockSpec(memory_space=pltpu.VMEM)
    smem = pl.BlockSpec(memory_space=pltpu.SMEM)
    count = 2 * (2 + 6 + 2 * (nz - 1) + 6 + 2) + 1
    count += (ny - 1) + 2 * (owners - 1) + (NX - 1) + (nz - 1)
    return pl.pallas_call(
        functools.partial(reduce_kernel, sizes),
        out_shape=(
            pltpu.VMEM((2, rows, cols), F32),
            pltpu.VMEM((2, 2 * rank, cols), BF16),
            pltpu.VMEM((rows, 2 * rank), F32),
            pltpu.VMEM((2, 2 * rank, 2 * rank), F32),
        ),
        in_specs=[hbm] * 6 + [smem],
        out_specs=(vmem,) * 4,
        scratch_shapes=[
            pltpu.VMEM((2, rows, cols), BF16),
            pltpu.VMEM((2, rows, cols), F32),
            pltpu.VMEM((2, rank, rows), F32),
            pltpu.VMEM((2, rows + rank, half), BF16),
            pltpu.VMEM((2, rows + rank, half), BF16),
            pltpu.VMEM((2, rank, half), F32),
            pltpu.VMEM((2, rank, half), F32),
            pltpu.VMEM((2, rank, half), F32),
            pltpu.VMEM((2, rows, half), F32),
            pltpu.VMEM((2, 2, group, half), F32),
            pltpu.VMEM((2, group, half), F32),
            pltpu.VMEM((2, nz, part_rows, part), F32),
            pltpu.VMEM((2, rank, cols), F32),
            pltpu.VMEM((rank, 2 * rank), F32),
            pltpu.VMEM((rank, 2 * rank), F32),
            pltpu.VMEM((ny, rank, 2 * rank), F32),
            pltpu.VMEM((rows, 2 * rank), F32),
            pltpu.VMEM((owners, share, 2 * rank), F32),
            pltpu.VMEM((NX, share, 2 * rank), F32),
            pltpu.VMEM((nz, share, 2 * rank), F32),
            pltpu.VMEM((rows, 2 * rank), F32),
            pltpu.VMEM((2, rank, 2 * rank), F32),
            pltpu.SemaphoreType.DMA((count,)),
            pltpu.SemaphoreType.DMA((count,)),
            pltpu.SemaphoreType.DMA((2, 2, 2, 2)),
            pltpu.SemaphoreType.DMA((2,)),
        ],
        compiler_params=pltpu.CompilerParams(
            collective_id=0,
            has_side_effects=True,
            vmem_limit_bytes=40 * 1024 * 1024,
        ),
        name="reduce_left",
    )(grad_in, grad_out, error_in, error_out, warm_in, warm_out, scale)


def finish_kernel(
    replicas,
    fields,
    left,
    prod,
    inv,
    new_error_in,
    new_error_out,
    new_warm_in,
    new_warm_out,
    factor,
    made,
    warms,
    store_sems,
    warm_sems,
):
    rows, cols = fields.shape[1:]
    rank = inv.shape[1] // 2
    tile = made.shape[-1]
    product = prod[...] * (1.0 / replicas)
    applied = exact(product, inv[1], 1, 0)
    lane = lax.broadcasted_iota(jnp.int32, (1, 2 * rank), 1)
    for m in range(2):
        own = jnp.where(lane // rank == m, applied, 0.0)
        moved = pltpu.roll(own, rank, 1)
        twice = (own + moved).astype(BF16)
        rest = halves((own, moved)[m])[1]
        factor[m] = jnp.concatenate([twice, rest], axis=1)
    stores = []
    for m, out in enumerate((new_error_in, new_error_out)):
        if m == 1:
            both = exact(inv[0], product, 1, 1)
            for n, warm_out in enumerate((new_warm_in, new_warm_out)):
                warms[n] = both[n * rank : (n + 1) * rank]
                store = pltpu.make_async_copy(
                    warms.at[n], warm_out, warm_sems.at[n]
                )
                store.start()
                stores.append(store)
        for t in range(cols // tile):
            c = pl.ds(t * tile, tile)
            stacked = jnp.concatenate([left[m, :, c], left[m, :, c]], axis=0)
            made[m, t] = fields[m, :, c] - dot(factor[m], stacked, 1, 0)
            store = pltpu.make_async_copy(
                made.at[m, t], out.at[:, c], store_sems.at[m, t]
            )
            store.start()
            stores.append(store)
    for store in stores:
        store.wait()


def finish_call(replicas, fields, left, prod, inv):
    rows, cols = fields.shape[1:]
    rank = inv.shape[1] // 2
    tile = min(512, cols)
    vmem = pl.BlockSpec(memory_space=pltpu.VMEM)
    hbm = pl.BlockSpec(memory_space=pltpu.HBM)
    return pl.pallas_call(
        functools.partial(finish_kernel, replicas),
        out_shape=(
            jax.ShapeDtypeStruct((rows, cols), F32),
            jax.ShapeDtypeStruct((rows, cols), F32),
            jax.ShapeDtypeStruct((rank, rows), F32),
            jax.ShapeDtypeStruct((rank, rows), F32),
        ),
        in_specs=[vmem] * 4,
        out_specs=(hbm,) * 4,
        scratch_shapes=[
            pltpu.VMEM((2, rows, 4 * rank), BF16),
            pltpu.VMEM((2, cols // tile, rows, tile), F32),
            pltpu.VMEM((2, rank, rows), F32),
            pltpu.SemaphoreType.DMA((2, cols // tile)),
            pltpu.SemaphoreType.DMA((2,)),
        ],
        compiler_params=pltpu.CompilerParams(
            vmem_limit_bytes=32 * 1024 * 1024,
        ),
        name="new_errors",
    )(fields, left, prod, inv)


def per_device(
    sizes, replicas, grad_in, grad_out, error_in, error_out, warm_in, warm_out, loss_scale
):
    wide = [
        pltpu.with_memory_space_constraint(a[0], pltpu.HBM)
        for a in (grad_in, grad_out, error_in, error_out)
    ]
    scale = loss_scale.reshape(1, 1)
    warms = [
        pltpu.with_memory_space_constraint(a.T, pltpu.HBM)
        for a in (warm_in, warm_out)
    ]
    reduced = reduce_call(sizes, *wide, *warms, scale)
    err_in, err_out, new_in, new_out = finish_call(replicas, *reduced)
    return err_in[None], err_out[None], new_in.T, new_out.T


def solution(mesh):
    wide = P("dp", None, "mp")
    sizes = (mesh.shape["mp"], mesh.shape["dp"] // (NX * CORES))
    return jax.shard_map(
        functools.partial(per_device, sizes, float(mesh.shape["dp"])),
        mesh=mesh,
        in_specs=(wide, wide, wide, wide, P(), P(), P()),
        out_specs=(wide, wide, P(), P()),
        check_vma=False,
    )
```
